512 devices in a mesh: ctx: 32 (over z_lo, x), kvh: 4 (over y), dp: 4 (over z_hi, core).
Axes of the slice: x: 4, y: 4, z: 16 (z_hi: 2, z_lo: 8; z = z_hi * 8 + z_lo), core: 2. Of those that a mesh axis runs over, the one named last changes fastest.
Arguments:
- queries: bfloat16 [4, 4096, 32, 128], P('dp', 'ctx', 'kvh'), may hold values from -4 to 4
- keys: bfloat16 [4, 4096, 4, 128], P('dp', 'ctx', 'kvh'), may hold values from -4 to 4
- values: bfloat16 [4, 4096, 4, 128], P('dp', 'ctx', 'kvh'), may hold values from -6 to 6
- d_out: bfloat16 [4, 4096, 32, 128], P('dp', 'ctx', 'kvh'), may hold values from -6 to 6
- head_scale: float32 [32], replicated, may hold values from 1 to 2
- doc_lengths: int32 [4, 16], P('dp'), may hold values from 1 to 2048, 4096 in all within a row
- span_order: int32 [64], replicated, may hold values from 0 to 63, each once
Outputs:
- out: bfloat16 [4, 4096, 32, 128], P('dp', 'ctx', 'kvh')
- d_queries: bfloat16 [4, 4096, 32, 128], P('dp', 'ctx', 'kvh')
- d_keys: bfloat16 [4, 4096, 4, 128], P('dp', 'ctx', 'kvh')
- d_values: bfloat16 [4, 4096, 4, 128], P('dp', 'ctx', 'kvh')
- d_head_scale: float32 [32], replicated
The draws below stay inside these ranges and needn't reach their ends.
Inputs may be any that keep to these rules, and one draw needn't show every extreme that they name: `doc_lengths`: each row sums to 4096; the longest document of each row reaches the maximum. `span_order`: each block number appears once.
All inputs are finite; a program needn't handle non-finite values.
Results may differ from the reference program's by a relative error of at most 0.03.
Values may be sent and summed in bfloat16 or wider, within the bound.
A program may use at most 64 MiB of HBM per device.

```python
import math
import jax
import jax.numpy as jnp
import numpy as np
from jax import lax

HD = 128
Q_PER_KV = 8
TOK_DEV = 128
DOCS = 16
KV_HEADS = 4
HEADS = 32
SEQ = 4096
SEQS = 4
SPANS = 64


def draw_keys(key, part):
    key = jax.random.fold_in(key, 5)
    drawn = jnp.clip(jax.random.normal(key, (SEQS, SEQ, KV_HEADS, HD), jnp.float32), -4.0, 4.0)
    return drawn.astype(jnp.bfloat16)


def draw_queries(key, part):
    key = jax.random.fold_in(key, 9)
    drawn = jnp.clip(jax.random.normal(key, (SEQS, SEQ, HEADS, HD), jnp.float32), -4.0, 4.0)
    return drawn.astype(jnp.bfloat16)


def steps_of(key, extent, cuts, low, largest):
    factor_of = 1.0
    for position, blocks in cuts:
        draws = jax.random.uniform(jax.random.fold_in(jax.random.fold_in(key, 6), position), (blocks,), jnp.float32, low / len(cuts), largest / len(cuts))
        factor_of = factor_of * jnp.repeat(jnp.exp(draws), extent[position] // blocks).reshape((-1,) + (1,) * (len(extent) - 1 - position))
    return factor_of


def split_up(amount, total, most, slope):
    portions = [(1 << 20) // math.isqrt(rank ** slope) + 1 for rank in range(2, amount + 1)]
    spare, holding = total - most - (amount - 1), [1] * (amount - 1)
    while spare > 0:
        movable = [i for i in range(amount - 1) if holding[i] < most]
        mass, left = sum([portions[i] for i in movable]), spare
        for i in movable:
            extra = min(most - holding[i], max(1, left * portions[i] // mass), spare)
            holding[i] = holding[i] + extra
            spare = spare - extra
    return np.array([most] + holding)


def uneven(key, amount, total, bound, lean):
    if amount == 2:
        one = jax.random.randint(key, (), max(1, total - bound), min(bound, total - 1) + 1)
        return jnp.stack([one, total - one])
    lengths = jnp.asarray(split_up(amount, total, bound, lean), jnp.int32)
    twos = (amount - 1) // 2
    giver, receiver = lengths[1:1 + 2 * twos:2], lengths[2:2 + 2 * twos:2]
    room = jnp.minimum(giver - 1, bound - receiver)
    moved = jax.random.randint(jax.random.fold_in(key, 1), (twos,), 0, 1 << 20) % (room + 1)
    lengths = lengths.at[1:1 + 2 * twos:2].set(giver - moved).at[2:2 + 2 * twos:2].set(receiver + moved)
    return lengths[jax.random.permutation(jax.random.fold_in(key, 2), amount)]


def noise(stream_key, shape, spread, most, shards=(), kind=jnp.bfloat16):
    entries = jax.random.normal(stream_key, shape, jnp.float32) * spread
    if len(shards) > 0:
        entries = steps_of(stream_key, shape, shards, -0.22, 0.18) * entries
    return jnp.clip(entries, min=-most, max=most).astype(kind)


def setup_inputs(seed: int = 0) -> dict:
    seeds = jax.random.split(jax.random.key(seed), 8)
    return {
        "queries": draw_queries(jax.random.fold_in(seeds[7], 71), 0),
        "keys": draw_keys(jax.random.fold_in(seeds[7], 71), 0),
        "values": noise(seeds[2], (SEQS, SEQ, KV_HEADS, HD), 1.0, 6.0, ((0, 4), (1, 32), (2, 4))),
        "d_out": noise(seeds[3], (SEQS, SEQ, HEADS, HD), 1.0, 6.0, ((0, 4), (1, 32), (2, 4))),
        "head_scale": jnp.clip(jnp.exp(jax.random.uniform(seeds[4], (HEADS,), jnp.float32, math.log(1.0), math.log(2.0))), 1.0, 2.0),
        "doc_lengths": jax.vmap(lambda own: uneven(own, DOCS, SEQ, SEQ // 2, 2))(jax.random.split(seeds[5], SEQS)).reshape((SEQS, DOCS)).astype(jnp.int32),
        "span_order": jax.random.permutation(seeds[6], SPANS).astype(jnp.int32),
    }


def span_places(span_order, row_ids, span_rows):
    return span_order[row_ids // span_rows] * span_rows + row_ids % span_rows

def document_ids(doc_row, places):
    bounds = jnp.cumsum(doc_row)
    return lax.optimization_barrier(jnp.sum((bounds[None, :] <= places[:, None]).astype(jnp.int32), axis=1))

def reference(queries, keys, values, d_out, head_scale, doc_lengths, span_order):
    span_rows = TOK_DEV // 2
    places = span_places(span_order, jnp.arange(SEQ, dtype=jnp.int32), span_rows)
    out_list, dq_list, dk_list, dv_list = ([], [], [], [])
    scale_grad = jnp.zeros((HEADS,), jnp.float32)
    for seq_index in range(SEQS):
        doc_ids = document_ids(doc_lengths[seq_index], places)
        visible = (doc_ids[:, None] == doc_ids[None, :]) & (places[None, :] <= places[:, None])
        group_outs, group_dqs, group_dks, group_dvs = ([], [], [], [])
        for group_index in range(KV_HEADS):
            key_rows = keys[seq_index, :, group_index, :]
            value_rows = values[seq_index, :, group_index, :]
            first = group_index * Q_PER_KV
            head_queries = jnp.moveaxis(queries[seq_index, :, first:first + Q_PER_KV, :], 1, 0)
            head_douts = jnp.moveaxis(d_out[seq_index, :, first:first + Q_PER_KV, :], 1, 0)
            head_scales = head_scale[first:first + Q_PER_KV]

            def one_head(carried, inputs):
                query_rows, dout_rows, scale_value = inputs
                factor = scale_value / math.sqrt(HD)
                raw_scores = jnp.dot(query_rows, key_rows.T, preferred_element_type=jnp.float32) * factor
                scores = jnp.where(visible, raw_scores, -jnp.inf)
                row_peak = lax.optimization_barrier(jnp.max(scores, axis=1))
                norm_log = row_peak + jnp.log(lax.optimization_barrier(jnp.sum(jnp.exp(scores - row_peak[:, None]), axis=1)))
                probs = jnp.exp(scores - norm_log[:, None]).astype(jnp.bfloat16)
                out_rows = jnp.dot(probs, value_rows, preferred_element_type=jnp.float32).astype(jnp.bfloat16)
                delta = lax.optimization_barrier(jnp.sum(dout_rows.astype(jnp.float32) * out_rows.astype(jnp.float32), axis=1))
                d_prob = jnp.dot(dout_rows, value_rows.T, preferred_element_type=jnp.float32)
                d_score = (probs.astype(jnp.float32) * (d_prob - delta[:, None])).astype(jnp.bfloat16)
                d_query = jnp.dot(d_score, key_rows, preferred_element_type=jnp.float32) * factor
                d_key = carried[0] + jnp.dot(d_score.T, query_rows, preferred_element_type=jnp.float32) * factor
                d_value = carried[1] + jnp.dot(probs.T, dout_rows, preferred_element_type=jnp.float32)
                centred = jnp.where(visible, raw_scores - norm_log[:, None], 0.0)
                grad_value = jnp.sum(d_score.astype(jnp.float32) * centred) / scale_value
                return ((d_key, d_value), (out_rows, d_query.astype(jnp.bfloat16), grad_value))
            start_grads = (jnp.zeros((SEQ, HD), jnp.float32), jnp.zeros((SEQ, HD), jnp.float32))
            (d_key, d_value), (head_outs, head_dqs, head_grads) = lax.scan(one_head, start_grads, (head_queries, head_douts, head_scales))
            group_outs.append(jnp.moveaxis(head_outs, 0, 1))
            group_dqs.append(jnp.moveaxis(head_dqs, 0, 1))
            group_dks.append(d_key.astype(jnp.bfloat16))
            group_dvs.append(d_value.astype(jnp.bfloat16))
            scale_grad = scale_grad.at[first:first + Q_PER_KV].add(head_grads)
        out_list.append(jnp.concatenate(group_outs, axis=1))
        dq_list.append(jnp.concatenate(group_dqs, axis=1))
        dk_list.append(jnp.stack(group_dks, axis=1))
        dv_list.append(jnp.stack(group_dvs, axis=1))
    return (jnp.stack(out_list), jnp.stack(dq_list), jnp.stack(dk_list), jnp.stack(dv_list), scale_grad)
```

```python
import functools
import math

import jax
import jax.numpy as jnp
from jax import lax
from jax.experimental import pallas as pl
from jax.experimental.pallas import tpu as pltpu
from jax.sharding import PartitionSpec as P

MESH = pl.DeviceIdType.MESH
masked_low = -1e30
NX = 4
ROW_TILE = 256


def nt_dot(a, b):
    return lax.dot_general(a, b, (((1,), (1,)), ((), ())), preferred_element_type=jnp.float32)


def nn_dot(a, b):
    return lax.dot_general(a, b, (((1,), (0,)), ((), ())), preferred_element_type=jnp.float32)


def xor_index(a, b, count):
    total, bit = 0, 1
    while bit < count:
        total = total + ((a // bit + b // bit) % 2) * bit
        bit *= 2
    return total


def kernel(
    nz, group, tok, hd, docs,
    q_hbm, k_hbm, v_hbm, do_hbm, scale_ref, docs_ref, span_ref,
    out_hbm, dq_ref, dk_ref, dv_ref, hs_ref,
    q_s, do_s, qt_s, dot_s, kv, s_s, dp_s, row_lo, row_hi, m_s, l_s, acc_s,
    out_s, p_s, ds_s, part, rxa, rxc, rz,
    in_sem, g_recv, g_send, a_recv, a_send, c_recv, c_send, z_recv, z_send,
):
    rows = group * tok
    chunk = NX * tok
    span = tok // 2
    me = lax.axis_index("ctx")
    z, x = me // NX, me % NX
    xr, xl, xo = (x + 1) % NX, (x + 3) % NX, (x + 2) % NX
    dev_xr, dev_xl = z * NX + xr, z * NX + xl
    dev_zr, dev_zl = ((z + 1) % nz) * NX + x, ((z + nz - 1) % nz) * NX + x

    k_in = pltpu.make_async_copy(k_hbm, kv.at[me, 0], in_sem.at[0])
    v_in = pltpu.make_async_copy(v_hbm, kv.at[me, 1], in_sem.at[1])
    q_in = pltpu.make_async_copy(q_hbm, q_s, in_sem.at[2])
    do_in = pltpu.make_async_copy(do_hbm, do_s, in_sem.at[3])
    for load in (k_in, v_in, q_in, do_in):
        load.start()

    barrier = pltpu.get_barrier_semaphore()
    for neighbour in (dev_xr, dev_xl, dev_zr, dev_zl):
        pl.semaphore_signal(barrier, inc=1, device_id={"ctx": neighbour}, device_id_type=MESH)
    pl.semaphore_wait(barrier, 4)

    def remote(src, dst, send_sem, recv_sem, device):
        return pltpu.make_async_remote_copy(
            src_ref=src,
            dst_ref=dst,
            send_sem=send_sem,
            recv_sem=recv_sem,
            device_id={"ctx": device},
            device_id_type=MESH,
        )

    def z_copy(origin, side):
        slot = origin * NX + x
        return remote(
            kv.at[slot],
            kv.at[slot],
            g_send.at[side, origin],
            g_recv.at[slot, 0],
            dev_zr if side == 0 else dev_zl,
        )

    def x_copy(j, origin_x, side):
        zb = xor_index(z, j, nz)
        slot = zb * NX + origin_x
        return remote(
            kv.at[slot],
            kv.at[slot],
            g_send.at[2 + side, j],
            g_recv.at[slot, 0],
            dev_xr if side == 0 else dev_xl,
        )

    def relay_copy(j, origin_x, side):
        zb = xor_index(z, j, nz)
        slot = zb * NX + origin_x
        return remote(
            kv.at[slot, side],
            kv.at[slot, side],
            g_send.at[4 + side, j],
            g_recv.at[slot, side],
            dev_xr if side == 0 else dev_xl,
        )

    k_in.wait()
    v_in.wait()

    @pl.when(z < nz - 1)
    def _():
        z_copy(z, 0).start()

    @pl.when(z > 0)
    def _():
        z_copy(z, 1).start()

    x_copy(0, x, 0).start()
    x_copy(0, x, 1).start()

    head0 = lax.axis_index("kvh") * group
    sub = lax.broadcasted_iota(jnp.int32, (group, hd), 0)
    scale8 = jnp.zeros((group, hd), jnp.float32)
    for h in range(group):
        scale8 = jnp.where(sub == h, scale_ref[head0 + h], scale8)
    factor8 = scale8 * (1.0 / math.sqrt(hd))

    def per_row(tile8):
        count = ROW_TILE // group
        return jnp.broadcast_to(tile8[None], (count, group, hd)).reshape(ROW_TILE, hd)

    bounds = []
    running = jnp.int32(0)
    for d in range(docs):
        running = running + docs_ref[0, d]
        bounds.append(running)
    first_span, second_span = span_ref[2 * me], span_ref[2 * me + 1]

    def row_values(r, carry):
        base = r * ROW_TILE
        token = (lax.broadcasted_iota(jnp.int32, (ROW_TILE, hd), 0) + base) // group
        place = jnp.where(token < span, first_span * span, second_span * span - span) + token
        low = jnp.zeros_like(place)
        for bound in bounds:
            low = jnp.maximum(low, jnp.where(place >= bound, bound, 0))
        at = pl.ds(pl.multiple_of(base, ROW_TILE), ROW_TILE)
        row_hi[at] = place
        row_lo[at] = low
        m_s[at] = jnp.full((ROW_TILE, hd), masked_low, jnp.float32)
        l_s[at] = jnp.zeros((ROW_TILE, hd), jnp.float32)
        acc_s[at] = jnp.zeros((ROW_TILE, hd), jnp.float32)
        return carry

    lax.fori_loop(0, rows // ROW_TILE, row_values, 0)
    q_in.wait()
    do_in.wait()
    for r in range(rows // ROW_TILE):
        at = slice(r * ROW_TILE, (r + 1) * ROW_TILE)
        qt_s[:, at] = q_s[at].astype(jnp.float32).T.astype(jnp.bfloat16)
        dot_s[:, at] = do_s[at].astype(jnp.float32).T.astype(jnp.bfloat16)

    def chunk_rows(zb, which):
        return kv[pl.ds(zb * NX, NX), which].reshape(chunk, hd)

    def forward_chunk(j):
        zb = xor_index(z, j, nz)
        key_rows, value_rows = chunk_rows(zb, 0), chunk_rows(zb, 1)
        lane = lax.broadcasted_iota(jnp.int32, (group, tok), 1)
        places = []
        for b in range(NX):
            lower = span_ref[(zb * NX + b) * 2] * span
            upper = span_ref[(zb * NX + b) * 2 + 1] * span - span
            place = jnp.where(lane < span, lower, upper) + lane
            count = ROW_TILE // group
            places.append(jnp.broadcast_to(place[None], (count, group, tok)).reshape(ROW_TILE, tok))
        factor = per_row(factor8)
        for r in range(rows // ROW_TILE):
            at = slice(r * ROW_TILE, (r + 1) * ROW_TILE)
            raw = nt_dot(q_s[at], key_rows)
            low, high = row_lo[at], row_hi[at]
            scores = []
            for b in range(NX):
                visible = (places[b] >= low) & (places[b] <= high)
                score = jnp.where(visible, raw[:, b * tok : (b + 1) * tok] * factor, masked_low)
                s_s[j, at, b * tok : (b + 1) * tok] = score
                scores.append(score)
            peak = jnp.maximum(
                jnp.maximum(scores[0], scores[1]), jnp.maximum(scores[2], scores[3])
            )
            old = m_s[at]
            new = jnp.maximum(old, jnp.max(peak, axis=1, keepdims=True))
            m_s[at] = new
            alpha = jnp.exp(old - new)
            weights = [jnp.exp(score - new) for score in scores]
            l_s[at] = l_s[at] * alpha + ((weights[0] + weights[1]) + (weights[2] + weights[3]))
            weight_bf = jnp.concatenate([w.astype(jnp.bfloat16) for w in weights], axis=1)
            acc_s[at] = acc_s[at] * alpha + nn_dot(weight_bf, value_rows)
            d_prob = nt_dot(do_s[at], value_rows)
            for b in range(NX):
                dp_s[j, at, b * tok : (b + 1) * tok] = d_prob[:, b * tok : (b + 1) * tok] * factor

    def gather_step(i, carry):
        @pl.when(i < nz - 1)
        def _():
            d = i + 1

            @pl.when(z - d >= 0)
            def _():
                copy = z_copy(z - d, 0)
                copy.wait_recv()

                @pl.when(z < nz - 1)
                def _():
                    copy.start()

            @pl.when(z + d < nz)
            def _():
                copy = z_copy(z + d, 1)
                copy.wait_recv()

                @pl.when(z > 0)
                def _():
                    copy.start()

            x_copy(i + 1, x, 0).start()
            x_copy(i + 1, x, 1).start()

        @pl.when(i < nz)
        def _():
            x_copy(i, xl, 0).wait_recv()
            relay_copy(i, xl, 0).start()
            x_copy(i, xr, 1).wait_recv()
            relay_copy(i, xr, 1).start()

        @pl.when(i > 0)
        def _():
            relay_copy(i - 1, xo, 0).wait_recv()
            relay_copy(i - 1, xo, 1).wait_recv()
            forward_chunk(i - 1)

        return carry

    lax.fori_loop(0, nz + 1, gather_step, 0)

    def finish_rows(r, carry):
        at = pl.ds(pl.multiple_of(r * ROW_TILE, ROW_TILE), ROW_TILE)
        total = jnp.sum(l_s[at], axis=1, keepdims=True)
        out_rows = (acc_s[at] / total).astype(jnp.bfloat16)
        out_s[at] = out_rows
        m_s[at] = m_s[at] + jnp.log(total)
        product = do_s[at].astype(jnp.float32) * out_rows.astype(jnp.float32)
        l_s[at] = jnp.sum(product, axis=1, keepdims=True) * per_row(factor8)
        acc_s[at] = jnp.zeros((ROW_TILE, hd), jnp.float32)
        return carry

    lax.fori_loop(0, rows // ROW_TILE, finish_rows, 0)
    out_copy = pltpu.make_async_copy(out_s, out_hbm, in_sem.at[0])
    out_copy.start()

    def a_copy(j, side):
        return remote(
            part.at[j, xo, side],
            rxa.at[j, side],
            a_send.at[side, j],
            a_recv.at[side, j],
            dev_xl if side == 0 else dev_xr,
        )

    def c_copy(j, side):
        return remote(
            part.at[j, xl if side == 0 else xr],
            rxc.at[j, side],
            c_send.at[side, j],
            c_recv.at[side, j],
            dev_xl if side == 0 else dev_xr,
        )

    def z_sum_copy(j, zb, side):
        return remote(
            part.at[j, x],
            rz.at[side, zb],
            z_send.at[side, zb],
            z_recv.at[side, zb],
            dev_zr if side == 0 else dev_zl,
        )

    def add_bf(a, b):
        return (a.astype(jnp.float32) + b.astype(jnp.float32)).astype(jnp.bfloat16)

    hs_ref[...] = jnp.zeros_like(hs_ref)

    def backward_chunk(j):
        zb = xor_index(z, j, nz)
        key_rows = chunk_rows(zb, 0)
        hs_total = hs_ref[...]
        for r in range(rows // ROW_TILE):
            at = slice(r * ROW_TILE, (r + 1) * ROW_TILE)
            norm, delta = m_s[at], l_s[at]
            for b in range(NX):
                cols = slice(b * tok, (b + 1) * tok)
                centred = s_s[j, at, cols] - norm
                prob = jnp.exp(centred)
                d_score = prob * (dp_s[j, at, cols] - delta)
                p_s[at, cols] = prob.astype(jnp.bfloat16)
                ds_s[at, cols] = d_score.astype(jnp.bfloat16)
                terms = (d_score * centred).reshape(ROW_TILE // group, group, tok)
                hs_total = hs_total + jnp.sum(terms, axis=0)
            acc_s[at] = acc_s[at] + nn_dot(ds_s[at], key_rows)
        hs_ref[...] = hs_total
        d_key = nn_dot(qt_s[...], ds_s[...])
        d_value = nn_dot(dot_s[...], p_s[...])
        for b in range(NX):
            cols = slice(b * tok, (b + 1) * tok)
            part[j, b, 0] = d_key[:, cols].astype(jnp.bfloat16)
            part[j, b, 1] = d_value[:, cols].astype(jnp.bfloat16)

    def scatter_step(k, carry):
        @pl.when(k < nz)
        def _():
            j = nz - 1 - k
            backward_chunk(j)
            a_copy(j, 0).start()
            a_copy(j, 1).start()

        @pl.when((k >= 1) & (k <= nz))
        def _():
            j = nz - k
            a_copy(j, 0).wait_recv()
            part[j, xl, 0] = add_bf(part[j, xl, 0], rxa[j, 0])
            c_copy(j, 0).start()
            a_copy(j, 1).wait_recv()
            part[j, xr, 1] = add_bf(part[j, xr, 1], rxa[j, 1])
            c_copy(j, 1).start()

        @pl.when(k >= 2)
        def _():
            j = nz + 1 - k
            c_copy(j, 0).wait_recv()
            c_copy(j, 1).wait_recv()
            total = part[j, x].astype(jnp.float32) + rxc[j, 0].astype(jnp.float32)
            total = total + rxc[j, 1].astype(jnp.float32)
            part[j, x] = total.astype(jnp.bfloat16)

            @pl.when(j > 0)
            def _():
                @pl.when(z + j < nz)
                def _():
                    zb = z + j
                    at = xor_index(z, zb, nz)

                    @pl.when(z > 0)
                    def _():
                        z_sum_copy(at, zb, 0).wait_recv()
                        part[at, x] = add_bf(part[at, x], rz[0, zb])

                    z_sum_copy(at, zb, 0).start()

                @pl.when(z - j >= 0)
                def _():
                    zb = z - j
                    at = xor_index(z, zb, nz)

                    @pl.when(z < nz - 1)
                    def _():
                        z_sum_copy(at, zb, 1).wait_recv()
                        part[at, x] = add_bf(part[at, x], rz[1, zb])

                    z_sum_copy(at, zb, 1).start()

        return carry

    lax.fori_loop(0, nz + 2, scatter_step, 0)

    for r in range(rows // ROW_TILE):
        at = slice(r * ROW_TILE, (r + 1) * ROW_TILE)
        dq_ref[at] = acc_s[at].astype(jnp.bfloat16)

    @pl.when(z > 0)
    def _():
        z_sum_copy(0, z, 0).wait_recv()
        part[0, x] = add_bf(part[0, x], rz[0, z])

    @pl.when(z < nz - 1)
    def _():
        z_sum_copy(0, z, 1).wait_recv()
        part[0, x] = add_bf(part[0, x], rz[1, z])

    dk_ref[...] = part[0, x, 0].astype(jnp.float32).T.astype(jnp.bfloat16)
    dv_ref[...] = part[0, x, 1].astype(jnp.float32).T.astype(jnp.bfloat16)

    def drain(j, carry):
        x_copy(j, x, 0).wait_send()
        x_copy(j, x, 1).wait_send()
        relay_copy(j, xl, 0).wait_send()
        relay_copy(j, xr, 1).wait_send()
        a_copy(j, 0).wait_send()
        a_copy(j, 1).wait_send()
        c_copy(j, 0).wait_send()
        c_copy(j, 1).wait_send()

        @pl.when((j <= z) & (z < nz - 1))
        def _():
            z_copy(j, 0).wait_send()

        @pl.when((j >= z) & (z > 0))
        def _():
            z_copy(j, 1).wait_send()

        @pl.when(j > z)
        def _():
            z_sum_copy(xor_index(z, j, nz), j, 0).wait_send()

        @pl.when(j < z)
        def _():
            z_sum_copy(xor_index(z, j, nz), j, 1).wait_send()

        return carry

    lax.fori_loop(0, nz, drain, 0)
    out_copy.wait()


def local(queries, keys, values, d_out, head_scale, doc_lengths, span_order):
    _, tok, group, hd = queries.shape
    ctx = lax.axis_size("ctx")
    nz = ctx // NX
    rows, chunk = tok * group, NX * tok
    bf, f32, i32 = jnp.bfloat16, jnp.float32, jnp.int32
    any_spec = pl.BlockSpec(memory_space=pl.ANY)
    vmem_spec = pl.BlockSpec(memory_space=pltpu.VMEM)
    smem_spec = pl.BlockSpec(memory_space=pltpu.SMEM)
    dma = pltpu.SemaphoreType.DMA
    out, dq, dk, dv, hs = pl.pallas_call(
        functools.partial(kernel, nz, group, tok, hd, doc_lengths.shape[1]),
        out_shape=(
            jax.ShapeDtypeStruct((rows, hd), bf),
            jax.ShapeDtypeStruct((rows, hd), bf),
            jax.ShapeDtypeStruct((tok, hd), bf),
            jax.ShapeDtypeStruct((tok, hd), bf),
            jax.ShapeDtypeStruct((group, tok), f32),
        ),
        in_specs=[any_spec] * 4 + [smem_spec] * 3,
        out_specs=(any_spec, vmem_spec, vmem_spec, vmem_spec, vmem_spec),
        scratch_shapes=[
            pltpu.VMEM((rows, hd), bf),
            pltpu.VMEM((rows, hd), bf),
            pltpu.VMEM((hd, rows), bf),
            pltpu.VMEM((hd, rows), bf),
            pltpu.VMEM((ctx, 2, tok, hd), bf),
            pltpu.VMEM((nz, rows, chunk), f32),
            pltpu.VMEM((nz, rows, chunk), f32),
            pltpu.VMEM((rows, hd), i32),
            pltpu.VMEM((rows, hd), i32),
            pltpu.VMEM((rows, hd), f32),
            pltpu.VMEM((rows, hd), f32),
            pltpu.VMEM((rows, hd), f32),
            pltpu.VMEM((rows, hd), bf),
            pltpu.VMEM((rows, chunk), bf),
            pltpu.VMEM((rows, chunk), bf),
            pltpu.VMEM((nz, NX, 2, hd, tok), bf),
            pltpu.VMEM((nz, 2, hd, tok), bf),
            pltpu.VMEM((nz, 2, 2, hd, tok), bf),
            pltpu.VMEM((2, nz, 2, hd, tok), bf),
            dma((4,)),
            dma((ctx, 2)),
            dma((6, nz)),
            dma((2, nz)),
            dma((2, nz)),
            dma((2, nz)),
            dma((2, nz)),
            dma((2, nz)),
            dma((2, nz)),
        ],
        compiler_params=pltpu.CompilerParams(
            collective_id=0, has_side_effects=True, vmem_limit_bytes=60 * 1024 * 1024
        ),
    )(
        queries.reshape(rows, hd),
        keys.reshape(tok, hd),
        values.reshape(tok, hd),
        d_out.reshape(rows, hd),
        head_scale,
        doc_lengths,
        span_order,
    )
    head_start = lax.axis_index("kvh") * group
    scales = lax.dynamic_slice_in_dim(head_scale, head_start, group)
    scale_terms = jnp.sum(hs, axis=1) * math.sqrt(hd) / (scales * scales)
    placed = lax.dynamic_update_slice_in_dim(
        jnp.zeros((head_scale.shape[0],), f32), scale_terms, head_start, 0
    )
    d_head_scale = lax.psum(placed, ("ctx", "kvh", "dp"))
    return (
        out.reshape(queries.shape),
        dq.reshape(queries.shape),
        dk.reshape(keys.shape),
        dv.reshape(values.shape),
        d_head_scale,
    )


def solution(mesh):
    return jax.shard_map(
        local,
        mesh=mesh,
        in_specs=(
            P("dp", "ctx", "kvh", None),
            P("dp", "ctx", "kvh", None),
            P("dp", "ctx", "kvh", None),
            P("dp", "ctx", "kvh", None),
            P(),
            P("dp", None),
            P(),
        ),
        out_specs=(
            P("dp", "ctx", "kvh", None),
            P("dp", "ctx", "kvh", None),
            P("dp", "ctx", "kvh", None),
            P("dp", "ctx", "kvh", None),
            P(),
        ),
        check_vma=False,
    )
```

```python
import functools
import math

import jax
import jax.numpy as jnp
from jax import lax
from jax.experimental import pallas as pl
from jax.experimental.pallas import tpu as pltpu
from jax.sharding import PartitionSpec as P

MESH = pl.DeviceIdType.MESH
masked_low = -1e30
NX = 4
X_LAG = 2


def nt_dot(a, b):
    return lax.dot_general(a, b, (((1,), (1,)), ((), ())), preferred_element_type=jnp.float32)


def nn_dot(a, b):
    return lax.dot_general(a, b, (((1,), (0,)), ((), ())), preferred_element_type=jnp.float32)


def xor_index(a, b, count):
    total, bit = 0, 1
    while bit < count:
        total = total + (lax.rem(lax.div(a, bit) + lax.div(b, bit), 2)) * bit
        bit *= 2
    return total


def kernel(
    group, tok, hd, docs, nk, nd,
    q_hbm, k_hbm, v_hbm, do_hbm, scale_ref, docs_ref, span_ref,
    out_hbm, dq_hbm, dk_ref, dv_ref, hs_ref,
    q_s, do_s, qt_s, dot_s, kv, s_s, dp_s, row_lo, row_hi, m_s, l_s, acc_s,
    out_s, dq_s, p_s, ds_s, part, rxa, rxc, rz, hx, hz, hd_s,
    in_sem, g_recv, gz_send, gx_send, gr_send, a_send, a_recv,
    c_send, c_recv, z_send, z_recv,
    hx_send, hx_recv, hz_send, hz_recv, hd_send, hd_recv,
):
    nz = lax.axis_size("ctx") // NX
    rows = group * tok
    chunk = NX * tok
    span = tok // 2
    tile = min(512, rows)
    tiles = rows // tile
    me = lax.axis_index("ctx")
    ki, di = lax.axis_index("kvh"), lax.axis_index("dp")
    z, x = lax.div(me, NX), lax.rem(me, NX)
    pair = lax.div(z, 2)
    zp = z + 1 - 2 * lax.rem(z, 2)
    xr, xl, xo = lax.rem(x + 1, NX), lax.rem(x + 3, NX), lax.rem(x + 2, NX)

    def row(j):
        return xor_index(z, jnp.int32(j), nz)

    def z_dev(j):
        return {"ctx": row(j) * NX + x}

    def x_dev(shift):
        return {"ctx": z * NX + lax.rem(x + shift, NX)}

    right, left = x_dev(1), x_dev(3)
    mate = {"ctx": zp * NX + x}
    up = {"ctx": lax.rem(z + 2, nz) * NX + x}
    down = {"ctx": lax.rem(z + nz - 2, nz) * NX + x}

    def far_dev(t):
        return {"kvh": (ki + t // nd) % nk, "dp": (di + t % nd) % nd}

    k_in = pltpu.make_async_copy(k_hbm, kv.at[z, x, 0], in_sem.at[0])
    v_in = pltpu.make_async_copy(v_hbm, kv.at[z, x, 1], in_sem.at[1])
    q_in = pltpu.make_async_copy(q_hbm, q_s, in_sem.at[2])
    do_in = pltpu.make_async_copy(do_hbm, do_s, in_sem.at[3])
    for load in (k_in, v_in, q_in, do_in):
        load.start()

    barrier = pltpu.get_barrier_semaphore()
    partners = [z_dev(j) for j in range(1, nz)] + [x_dev(s) for s in range(1, NX)]
    partners = partners + [far_dev(t) for t in range(1, nk * nd)]
    for partner in partners:
        pl.semaphore_signal(barrier, inc=1, device_id=partner, device_id_type=MESH)
    pl.semaphore_wait(barrier, len(partners))

    def remote(src, dst, send_sem, recv_sem, device):
        return pltpu.make_async_remote_copy(
            src_ref=src,
            dst_ref=dst,
            send_sem=send_sem,
            recv_sem=recv_sem,
            device_id=device,
            device_id_type=MESH,
        )

    def block_copy(at, send_sem, device):
        return remote(kv.at[at], kv.at[at], send_sem, g_recv.at[at[0], at[1], 0], device)

    def line_copy(origin, side):
        return block_copy((origin, x), gz_send.at[side, origin], up if side == 0 else down)

    def mate_copy(origin):
        return block_copy((origin, x), gz_send.at[2, origin], mate)

    def x_copy(zb, bx, side):
        return block_copy((zb, bx), gx_send.at[side, zb], right if side == 0 else left)

    def relay_copy(zb, bx, side):
        at = (zb, bx, side)
        return remote(
            kv.at[at], kv.at[at], gr_send.at[side, zb], g_recv.at[at], right if side == 0 else left
        )

    def x_sends(zb):
        x_copy(zb, x, 0).start()
        x_copy(zb, x, 1).start()

    def relays(zb):
        x_copy(zb, xl, 0).wait_recv()
        relay_copy(zb, xl, 0).start()
        x_copy(zb, xr, 1).wait_recv()
        relay_copy(zb, xr, 1).start()

    def row_waits(zb):
        relay_copy(zb, xo, 0).wait_recv()
        relay_copy(zb, xo, 1).wait_recv()

    def forward_line(origin, side):
        @pl.when((z < nz - 2) if side == 0 else (z >= 2))
        def _():
            line_copy(origin, side).start()

    def line_step(e):
        if e < nz // 2:

            @pl.when(z >= 2 * e)
            def _():
                line_copy(z - 2 * e, 0).wait_recv()
                forward_line(z - 2 * e, 0)
                mate_copy(z - 2 * e).start()

            @pl.when(z + 2 * e < nz)
            def _():
                line_copy(z + 2 * e, 1).wait_recv()
                forward_line(z + 2 * e, 1)
                mate_copy(z + 2 * e).start()

        if e == 1:
            mate_copy(zp).wait_recv()
        else:

            @pl.when(zp >= 2 * (e - 1))
            def _():
                mate_copy(zp - 2 * (e - 1)).wait_recv()

            @pl.when(zp + 2 * (e - 1) < nz)
            def _():
                mate_copy(zp + 2 * (e - 1)).wait_recv()

    k_in.wait()
    v_in.wait()
    forward_line(z, 0)
    forward_line(z, 1)
    mate_copy(z).start()
    x_sends(z)

    head0 = ki * group
    sub = lax.broadcasted_iota(jnp.int32, (group, hd), 0)
    scale8 = jnp.zeros((group, hd), jnp.float32)
    for h in range(group):
        scale8 = jnp.where(sub == h, scale_ref[head0 + h], scale8)
    factor8 = scale8 * (1.0 / math.sqrt(hd))

    def per_row(tile8):
        return jnp.broadcast_to(tile8[None], (tile // group, group, hd)).reshape(tile, hd)

    bounds = []
    running = jnp.int32(0)
    for d in range(docs):
        running = running + docs_ref[0, d]
        bounds.append(running)
    first_span, second_span = span_ref[2 * me], span_ref[2 * me + 1]

    def row_values(r, carry):
        base = r * tile
        token = (lax.broadcasted_iota(jnp.int32, (tile, hd), 0) + base) // group
        place = jnp.where(token < span, first_span * span, second_span * span - span) + token
        low = jnp.zeros_like(place)
        for bound in bounds:
            low = jnp.maximum(low, jnp.where(place >= bound, bound, 0))
        at = pl.ds(pl.multiple_of(base, tile), tile)
        row_hi[at] = place
        row_lo[at] = low
        m_s[at] = jnp.full((tile, hd), masked_low, jnp.float32)
        l_s[at] = jnp.zeros((tile, hd), jnp.float32)
        acc_s[at] = jnp.zeros((tile, hd), jnp.float32)
        return carry

    lax.fori_loop(0, tiles, row_values, 0)
    q_in.wait()
    do_in.wait()

    def chunk_rows(zb, which):
        return kv[zb, :, which].reshape(chunk, hd)

    def forward_chunk(i, zb):
        key_rows, value_rows = chunk_rows(zb, 0), chunk_rows(zb, 1)
        lane = lax.broadcasted_iota(jnp.int32, (group, tok), 1)
        places = []
        for b in range(NX):
            owner = zb * NX + b
            lower = span_ref[owner * 2] * span
            upper = span_ref[owner * 2 + 1] * span - span
            place = jnp.where(lane < span, lower, upper) + lane
            places.append(
                jnp.broadcast_to(place[None], (tile // group, group, tok)).reshape(tile, tok)
            )
        factor = per_row(factor8)
        for r in range(tiles):
            at = slice(r * tile, (r + 1) * tile)
            raw = nt_dot(q_s[at], key_rows)
            low, high = row_lo[at], row_hi[at]
            scores = []
            for b in range(NX):
                visible = (places[b] >= low) & (places[b] <= high)
                score = jnp.where(visible, raw[:, b * tok : (b + 1) * tok] * factor, masked_low)
                s_s[i, at, b * tok : (b + 1) * tok] = score
                scores.append(score)
            peak = jnp.maximum(
                jnp.maximum(scores[0], scores[1]), jnp.maximum(scores[2], scores[3])
            )
            old = m_s[at]
            new = jnp.maximum(old, jnp.max(peak, axis=1, keepdims=True))
            m_s[at] = new
            alpha = jnp.exp(old - new)
            weights = [jnp.exp(score - new) for score in scores]
            l_s[at] = l_s[at] * alpha + ((weights[0] + weights[1]) + (weights[2] + weights[3]))
            for b in range(NX):
                p_s[at, b * tok : (b + 1) * tok] = weights[b].astype(jnp.bfloat16)
            acc_s[at] = acc_s[at] * alpha
            d_prob = nt_dot(do_s[at], value_rows)
            for b in range(NX):
                dp_s[i, at, b * tok : (b + 1) * tok] = d_prob[:, b * tok : (b + 1) * tok] * factor
        acc_s[...] = acc_s[...] + nn_dot(p_s[...], value_rows)

    def gather_step(i, carry):
        for e in range(1, nz // 2 + 1):

            @pl.when(i == 2 * e - 1)
            def _():
                line_step(e)

        @pl.when((i > 0) & (i < nz))
        def _():
            x_sends(row(i))

        @pl.when((i >= X_LAG) & (i < nz + X_LAG))
        def _():
            relays(row(i - X_LAG))

        @pl.when(i >= 2 * X_LAG)
        def _():
            zb = row(i - 2 * X_LAG)
            row_waits(zb)
            forward_chunk(i - 2 * X_LAG, zb)

        return carry

    lax.fori_loop(0, nz + 2 * X_LAG, gather_step, 0)

    def finish_rows(r, carry):
        at = pl.ds(pl.multiple_of(r * tile, tile), tile)
        total = jnp.sum(l_s[at], axis=1, keepdims=True)
        out_rows = (acc_s[at] / total).astype(jnp.bfloat16)
        out_s[at] = out_rows
        m_s[at] = m_s[at] + jnp.log(total)
        product = do_s[at].astype(jnp.float32) * out_rows.astype(jnp.float32)
        l_s[at] = jnp.sum(product, axis=1, keepdims=True) * per_row(factor8)
        acc_s[at] = jnp.zeros((tile, hd), jnp.float32)
        return carry

    lax.fori_loop(0, tiles, finish_rows, 0)
    out_copy = pltpu.make_async_copy(out_s, out_hbm, in_sem.at[0])
    out_copy.start()
    for r in range(tiles):
        at = slice(r * tile, (r + 1) * tile)
        qt_s[:, at] = q_s[at].astype(jnp.float32).T.astype(jnp.bfloat16)
        dot_s[:, at] = do_s[at].astype(jnp.float32).T.astype(jnp.bfloat16)

    def a_copy(j, side):
        return remote(
            part.at[j, xo, side],
            rxa.at[j, side],
            a_send.at[j, side],
            a_recv.at[j, side],
            left if side == 0 else right,
        )

    def c_copy(j, side, piece):
        return remote(
            part.at[j, xl if side == 0 else xr, piece],
            rxc.at[j, side, piece],
            c_send.at[j, side, piece],
            c_recv.at[j, side, piece],
            left if side == 0 else right,
        )

    def line_sum(j, zb, side):
        return remote(
            part.at[j, x], rz.at[side, zb], z_send.at[side, zb], z_recv.at[side, zb],
            up if side == 0 else down,
        )

    def mate_sum(j, zb):
        return remote(part.at[j, x], rz.at[2, zb], z_send.at[2, zb], z_recv.at[2, zb], mate)

    def add_bf(a, b):
        return (a.astype(jnp.float32) + b.astype(jnp.float32)).astype(jnp.bfloat16)

    def neighbour_sums(j):
        a_copy(j, 0).wait_recv()
        part[j, xl, 0] = add_bf(part[j, xl, 0], rxa[j, 0])
        c_copy(j, 0, 0).start()
        a_copy(j, 1).wait_recv()
        part[j, xr, 1] = add_bf(part[j, xr, 1], rxa[j, 1])
        c_copy(j, 1, 1).start()

    def column_sums(j):
        for side in range(2):
            for piece in range(2):
                c_copy(j, side, piece).wait_recv()
        total = part[j, x].astype(jnp.float32) + rxc[j, 0].astype(jnp.float32)
        total = total + rxc[j, 1].astype(jnp.float32)
        part[j, x] = total.astype(jnp.bfloat16)

    def to_mate(s):
        def send(target):
            mate_sum(2 * xor_index(pair, target, nz // 2) + 1, zp + 2 * (target - pair)).start()

        if s == 0:
            send(pair)
        else:

            @pl.when(pair + s < nz // 2)
            def _():
                send(pair + s)

            @pl.when(pair >= s)
            def _():
                send(pair - s)

    def along_line(s):
        @pl.when(pair + s < nz // 2)
        def _():
            zb = z + 2 * s
            at = 2 * xor_index(pair, pair + s, nz // 2)
            mate_sum(at, zb).wait_recv()
            part[at, x] = add_bf(part[at, x], rz[2, zb])

            @pl.when(pair > 0)
            def _():
                line_sum(at, zb, 0).wait_recv()
                part[at, x] = add_bf(part[at, x], rz[0, zb])

            line_sum(at, zb, 0).start()

        @pl.when(pair >= s)
        def _():
            zb = z - 2 * s
            at = 2 * xor_index(pair, pair - s, nz // 2)
            mate_sum(at, zb).wait_recv()
            part[at, x] = add_bf(part[at, x], rz[2, zb])

            @pl.when(pair < nz // 2 - 1)
            def _():
                line_sum(at, zb, 1).wait_recv()
                part[at, x] = add_bf(part[at, x], rz[1, zb])

            line_sum(at, zb, 1).start()

    hs_ref[...] = jnp.zeros_like(hs_ref)
    hx[x] = jnp.zeros((group, tok), jnp.float32)

    def backward_chunk(i):
        key_rows = chunk_rows(row(i), 0)
        hs_total = hx[x]
        for r in range(tiles):
            at = slice(r * tile, (r + 1) * tile)
            norm, delta = m_s[at], l_s[at]
            for b in range(NX):
                cols = slice(b * tok, (b + 1) * tok)
                centred = s_s[i, at, cols] - norm
                prob = jnp.exp(centred)
                d_score = prob * (dp_s[i, at, cols] - delta)
                p_s[at, cols] = prob.astype(jnp.bfloat16)
                ds_s[at, cols] = d_score.astype(jnp.bfloat16)
                terms = (d_score * centred).reshape(tile // group, group, tok)
                hs_total = hs_total + jnp.sum(terms, axis=0)
            acc_s[at] = acc_s[at] + nn_dot(ds_s[at], key_rows)
        hx[x] = hs_total
        d_key = nn_dot(qt_s[...], ds_s[...])
        d_value = nn_dot(dot_s[...], p_s[...])
        for b in range(NX):
            cols = slice(b * tok, (b + 1) * tok)
            part[i, b, 0] = d_key[:, cols].astype(jnp.bfloat16)
            part[i, b, 1] = d_value[:, cols].astype(jnp.bfloat16)

    def hx_copy(s):
        return remote(
            hx.at[x], hx.at[x], hx_send.at[s], hx_recv.at[x], x_dev(s)
        )

    def hz_copy(j):
        return remote(hz.at[z], hz.at[z], hz_send.at[j], hz_recv.at[z], z_dev(j))

    def far_copy(t):
        slot = ki * nd + di
        return remote(hd_s.at[slot], hd_s.at[slot], hd_send.at[t], hd_recv.at[slot], far_dev(t))

    def arrived(buffer, sems, slot):
        remote(buffer.at[slot], buffer.at[slot], sems.at[slot], sems.at[slot], x_dev(1)).wait_recv()

    def scatter_step(k, carry):
        @pl.when(k < nz)
        def _():
            j = nz - 1 - k
            backward_chunk(j)
            a_copy(j, 0).start()
            a_copy(j, 1).start()
            c_copy(j, 0, 1).start()
            c_copy(j, 1, 0).start()

        @pl.when(k == nz - 1)
        def _():
            for s in range(1, NX):
                hx_copy(s).start()
            for r in range(tiles):
                at = slice(r * tile, (r + 1) * tile)
                dq_s[at] = acc_s[at].astype(jnp.bfloat16)
            dq_copy.start()

        @pl.when((k >= X_LAG) & (k < nz + X_LAG))
        def _():
            neighbour_sums(nz - 1 - k + X_LAG)

        @pl.when(k >= 2 * X_LAG)
        def _():
            j = nz - 1 - k + 2 * X_LAG
            column_sums(j)

        for f in range(nz // 2):

            @pl.when(k == 2 * X_LAG + 2 * f)
            def _():
                if f > 0:
                    along_line(nz // 2 - f)
                to_mate(nz // 2 - 1 - f)

        @pl.when(k == nz)
        def _():
            for s in range(1, NX):
                arrived(hx, hx_recv, (x + s) % NX)
            hz[z] = (hx[0] + hx[1]) + (hx[2] + hx[3])
            for j in range(1, nz):
                hz_copy(j).start()

        @pl.when(k == nz + 2)
        def _():
            for j in range(1, nz):
                arrived(hz, hz_recv, row(j))
            hs_line = hz[0]
            for j in range(1, nz):
                hs_line = hs_line + hz[j]
            hd_s[ki * nd + di] = hs_line
            for t in range(1, nk * nd):
                far_copy(t).start()

        return carry

    dq_copy = pltpu.make_async_copy(dq_s, dq_hbm, in_sem.at[1])
    lax.fori_loop(0, nz + 2 * X_LAG, scatter_step, 0)

    total = part[0, x].astype(jnp.float32)
    mate_sum(0, z).wait_recv()
    rz_own = rz[2, z].astype(jnp.float32)
    part[0, x] = (total + rz_own).astype(jnp.bfloat16)

    @pl.when(pair > 0)
    def _():
        line_sum(0, z, 0).wait_recv()
        part[0, x] = add_bf(part[0, x], rz[0, z])

    @pl.when(pair < nz // 2 - 1)
    def _():
        line_sum(0, z, 1).wait_recv()
        part[0, x] = add_bf(part[0, x], rz[1, z])

    dk_ref[...] = part[0, x, 0].astype(jnp.float32).T.astype(jnp.bfloat16)
    dv_ref[...] = part[0, x, 1].astype(jnp.float32).T.astype(jnp.bfloat16)

    for t in range(1, nk * nd):
        arrived(hd_s, hd_recv, ((ki + t // nd) % nk) * nd + (di + t % nd) % nd)
    for kk in range(nk):
        head_total = hd_s[kk * nd]
        for dd in range(1, nd):
            head_total = head_total + hd_s[kk * nd + dd]
        hs_ref[kk * group : (kk + 1) * group] = head_total

    for s in range(1, NX):
        hx_copy(s).wait_send()
    for j in range(1, nz):
        hz_copy(j).wait_send()
    for t in range(1, nk * nd):
        far_copy(t).wait_send()

    def drain(j, carry):
        for side in range(2):
            x_copy(j, x, side).wait_send()
            relay_copy(j, xl, side).wait_send()
            a_copy(j, side).wait_send()
            for piece in range(2):
                c_copy(j, side, piece).wait_send()
        same = lax.rem(z + j, 2) == 0

        @pl.when(same)
        def _():
            mate_copy(j).wait_send()

            @pl.when((j <= z) & (z < nz - 2))
            def _():
                line_copy(j, 0).wait_send()

            @pl.when((j >= z) & (z >= 2))
            def _():
                line_copy(j, 1).wait_send()

            @pl.when(j > z)
            def _():
                line_sum(0, j, 0).wait_send()

            @pl.when(j < z)
            def _():
                line_sum(0, j, 1).wait_send()

        @pl.when(jnp.logical_not(same))
        def _():
            mate_sum(0, j).wait_send()

        return carry

    lax.fori_loop(0, nz, drain, 0)
    out_copy.wait()
    dq_copy.wait()


def local(queries, keys, values, d_out, head_scale, doc_lengths, span_order):
    _, tok, group, hd = queries.shape
    nz = lax.axis_size("ctx") // NX
    nk, nd = lax.axis_size("kvh"), lax.axis_size("dp")
    rows, chunk = tok * group, NX * tok
    bf, f32, i32 = jnp.bfloat16, jnp.float32, jnp.int32
    any_spec = pl.BlockSpec(memory_space=pl.ANY)
    vmem_spec = pl.BlockSpec(memory_space=pltpu.VMEM)
    smem_spec = pl.BlockSpec(memory_space=pltpu.SMEM)
    dma = pltpu.SemaphoreType.DMA
    out, dq, dk, dv, hs = pl.pallas_call(
        functools.partial(kernel, group, tok, hd, doc_lengths.shape[1], nk, nd),
        out_shape=(
            jax.ShapeDtypeStruct((rows, hd), bf),
            jax.ShapeDtypeStruct((rows, hd), bf),
            jax.ShapeDtypeStruct((tok, hd), bf),
            jax.ShapeDtypeStruct((tok, hd), bf),
            jax.ShapeDtypeStruct((nk * group, tok), f32),
        ),
        in_specs=[any_spec] * 4 + [smem_spec] * 3,
        out_specs=(any_spec, any_spec, vmem_spec, vmem_spec, vmem_spec),
        scratch_shapes=[
            pltpu.VMEM((rows, hd), bf),
            pltpu.VMEM((rows, hd), bf),
            pltpu.VMEM((hd, rows), bf),
            pltpu.VMEM((hd, rows), bf),
            pltpu.VMEM((nz, NX, 2, tok, hd), bf),
            pltpu.VMEM((nz, rows, chunk), f32),
            pltpu.VMEM((nz, rows, chunk), f32),
            pltpu.VMEM((rows, hd), i32),
            pltpu.VMEM((rows, hd), i32),
            pltpu.VMEM((rows, hd), f32),
            pltpu.VMEM((rows, hd), f32),
            pltpu.VMEM((rows, hd), f32),
            pltpu.VMEM((rows, hd), bf),
            pltpu.VMEM((rows, hd), bf),
            pltpu.VMEM((rows, chunk), bf),
            pltpu.VMEM((rows, chunk), bf),
            pltpu.VMEM((nz, NX, 2, hd, tok), bf),
            pltpu.VMEM((nz, 2, hd, tok), bf),
            pltpu.VMEM((nz, 2, 2, hd, tok), bf),
            pltpu.VMEM((3, nz, 2, hd, tok), bf),
            pltpu.VMEM((NX, group, tok), f32),
            pltpu.VMEM((nz, group, tok), f32),
            pltpu.VMEM((nk * nd, group, tok), f32),
            dma((4,)),
            dma((nz, NX, 2)),
            dma((3, nz)),
            dma((2, nz)),
            dma((2, nz)),
            dma((nz, 2)),
            dma((nz, 2)),
            dma((nz, 2, 2)),
            dma((nz, 2, 2)),
            dma((3, nz)),
            dma((3, nz)),
            dma((NX,)),
            dma((NX,)),
            dma((nz,)),
            dma((nz,)),
            dma((nk * nd,)),
            dma((nk * nd,)),
        ],
        compiler_params=pltpu.CompilerParams(
            collective_id=0, has_side_effects=True, vmem_limit_bytes=60 * 1024 * 1024
        ),
    )(
        queries.reshape(rows, hd),
        keys.reshape(tok, hd),
        values.reshape(tok, hd),
        d_out.reshape(rows, hd),
        head_scale,
        doc_lengths,
        span_order,
    )
    d_head_scale = jnp.sum(hs, axis=1) * math.sqrt(hd) / (head_scale * head_scale)
    return (
        out.reshape(queries.shape),
        dq.reshape(queries.shape),
        dk.reshape(keys.shape),
        dv.reshape(values.shape),
        d_head_scale,
    )


def solution(mesh):
    return jax.shard_map(
        local,
        mesh=mesh,
        in_specs=(
            P("dp", "ctx", "kvh", None),
            P("dp", "ctx", "kvh", None),
            P("dp", "ctx", "kvh", None),
            P("dp", "ctx", "kvh", None),
            P(),
            P("dp", None),
            P(),
        ),
        out_specs=(
            P("dp", "ctx", "kvh", None),
            P("dp", "ctx", "kvh", None),
            P("dp", "ctx", "kvh", None),
            P("dp", "ctx", "kvh", None),
            P(),
        ),
        check_vma=False,
    )
```

```python
import functools
import math

import jax
import jax.numpy as jnp
from jax import lax
from jax.experimental import pallas as pl
from jax.experimental.pallas import tpu as pltpu
from jax.sharding import PartitionSpec as P

MESH = pl.DeviceIdType.MESH
masked_low = -1e30
NX = 4
X_LAG = 2


def nt_dot(a, b):
    return lax.dot_general(a, b, (((1,), (1,)), ((), ())), preferred_element_type=jnp.float32)


def nn_dot(a, b):
    return lax.dot_general(a, b, (((1,), (0,)), ((), ())), preferred_element_type=jnp.float32)


def xor_index(a, b, count):
    total, bit = 0, 1
    while bit < count:
        total = total + (lax.rem(lax.div(a, bit) + lax.div(b, bit), 2)) * bit
        bit *= 2
    return total


def kernel(
    group, tok, hd, docs, nk, nd,
    q_hbm, k_hbm, v_hbm, do_hbm, scale_ref, docs_ref, span_ref,
    out_hbm, dq_hbm, dk_ref, dv_ref, hs_ref,
    q_s, do_s, qt_s, dot_s, kv, s_s, dp_s, row_lo, row_hi, m_s, l_s, wu_s, wd_s, wdu_s, acc_s,
    out_s, dq_s, p_s, ds_s, part, rxa, rxc, rz, h_own, h_kv, h_plane, h_own_all, h_line, h_gate, h_hi, h_all,
    in_sem, g_recv, gz_send, gx_send, gr_send, a_send, a_recv,
    c_send, c_recv, z_send, z_recv,
    h_send, hk_recv, hp_recv, hl_recv, hh_recv, ha_recv,
):
    nz = lax.axis_size("ctx") // NX
    rows = group * tok
    chunk = NX * tok
    span = tok // 2
    tile = min(512, rows)
    tiles = rows // tile
    me = lax.axis_index("ctx")
    ki, di = lax.axis_index("kvh"), lax.axis_index("dp")
    z, x = lax.div(me, NX), lax.rem(me, NX)
    pair = lax.div(z, 2)
    zp = z + 1 - 2 * lax.rem(z, 2)
    xr, xl, xo = lax.rem(x + 1, NX), lax.rem(x + 3, NX), lax.rem(x + 2, NX)

    def row(j):
        return xor_index(z, jnp.int32(j), nz)

    def x_dev(shift):
        return {"ctx": z * NX + lax.rem(x + shift, NX)}

    right, left = x_dev(1), x_dev(3)
    mate = {"ctx": zp * NX + x}
    up = {"ctx": lax.rem(z + 2, nz) * NX + x}
    down = {"ctx": lax.rem(z + nz - 2, nz) * NX + x}

    cores = min(2, nd)
    core, hi = lax.rem(di, cores), lax.div(di, cores)
    gate = (nz - 1) * (1 - hi)
    at_gate = z == gate

    def kv_dev(t):
        return {"kvh": lax.rem(ki + t, nk)}

    def plane_dev(t):
        to_core = lax.rem(core + t // NX, cores)
        return {"ctx": z * NX + lax.rem(x + t % NX, NX), "dp": hi * cores + to_core}

    def line_dev(zz):
        return {"ctx": zz * NX + x}

    across = {"ctx": (nz - 1) * hi * NX + x, "dp": lax.rem(di + cores, nd)}

    k_in = pltpu.make_async_copy(k_hbm, kv.at[z, x, 0], in_sem.at[0])
    v_in = pltpu.make_async_copy(v_hbm, kv.at[z, x, 1], in_sem.at[1])
    q_in = pltpu.make_async_copy(q_hbm, q_s, in_sem.at[2])
    do_in = pltpu.make_async_copy(do_hbm, do_s, in_sem.at[3])
    for load in (k_in, v_in, q_in, do_in):
        load.start()

    barrier = pltpu.get_barrier_semaphore()
    partners = [mate] + [kv_dev(t) for t in range(1, nk)]
    partners = partners + [plane_dev(t) for t in range(1, NX * cores)]

    def greet(partner):
        pl.semaphore_signal(barrier, inc=1, device_id=partner, device_id_type=MESH)

    for partner in partners:
        greet(partner)

    @pl.when(z < nz - 2)
    def _():
        greet(up)

    @pl.when(z >= 2)
    def _():
        greet(down)

    inner = jnp.where((z >= 2) & (z < nz - 2), 1, 0)
    if nd > cores:

        @pl.when(at_gate)
        def _():
            greet(across)

        inner = inner + jnp.where(at_gate, 1, 0)
    pl.semaphore_wait(barrier, len(partners) + 1 + inner)

    def remote(src, dst, send_sem, recv_sem, device):
        return pltpu.make_async_remote_copy(
            src_ref=src,
            dst_ref=dst,
            send_sem=send_sem,
            recv_sem=recv_sem,
            device_id=device,
            device_id_type=MESH,
        )

    def block_copy(at, send_sem, device):
        return remote(kv.at[at], kv.at[at], send_sem, g_recv.at[at[0], at[1], 0], device)

    def line_copy(origin, side):
        return block_copy((origin, x), gz_send.at[side, origin], up if side == 0 else down)

    def mate_copy(origin):
        return block_copy((origin, x), gz_send.at[2, origin], mate)

    def x_copy(zb, bx, side):
        return block_copy((zb, bx), gx_send.at[side, zb], right if side == 0 else left)

    def relay_copy(zb, bx, side):
        at = (zb, bx, side)
        return remote(
            kv.at[at], kv.at[at], gr_send.at[side, zb], g_recv.at[at], right if side == 0 else left
        )

    def x_sends(zb):
        x_copy(zb, x, 0).start()
        x_copy(zb, x, 1).start()

    def relays(zb):
        x_copy(zb, xl, 0).wait_recv()
        relay_copy(zb, xl, 0).start()
        x_copy(zb, xr, 1).wait_recv()
        relay_copy(zb, xr, 1).start()

    def row_waits(zb):
        relay_copy(zb, xo, 0).wait_recv()
        relay_copy(zb, xo, 1).wait_recv()

    def forward_line(origin, side):
        @pl.when((z < nz - 2) if side == 0 else (z >= 2))
        def _():
            line_copy(origin, side).start()

    def line_step(e):
        if e < nz // 2:

            @pl.when(z >= 2 * e)
            def _():
                line_copy(z - 2 * e, 0).wait_recv()
                forward_line(z - 2 * e, 0)
                mate_copy(z - 2 * e).start()

            @pl.when(z + 2 * e < nz)
            def _():
                line_copy(z + 2 * e, 1).wait_recv()
                forward_line(z + 2 * e, 1)
                mate_copy(z + 2 * e).start()

        if e == 1:
            mate_copy(zp).wait_recv()
        else:

            @pl.when(zp >= 2 * (e - 1))
            def _():
                mate_copy(zp - 2 * (e - 1)).wait_recv()

            @pl.when(zp + 2 * (e - 1) < nz)
            def _():
                mate_copy(zp + 2 * (e - 1)).wait_recv()

    k_in.wait()
    v_in.wait()
    forward_line(z, 0)
    forward_line(z, 1)
    mate_copy(z).start()
    x_sends(z)

    head0 = ki * group
    sub = lax.broadcasted_iota(jnp.int32, (group, hd), 0)
    scale8 = jnp.zeros((group, hd), jnp.float32)
    for h in range(group):
        scale8 = jnp.where(sub == h, scale_ref[head0 + h], scale8)
    factor8 = scale8 * (1.0 / math.sqrt(hd))

    def per_row(tile8):
        return jnp.broadcast_to(tile8[None], (tile // group, group, hd)).reshape(tile, hd)

    bounds = []
    running = jnp.int32(0)
    for d in range(docs):
        running = running + docs_ref[0, d]
        bounds.append(running)
    first_span, second_span = span_ref[2 * me], span_ref[2 * me + 1]

    def row_values(r, carry):
        base = r * tile
        token = (lax.broadcasted_iota(jnp.int32, (tile, hd), 0) + base) // group
        place = jnp.where(token < span, first_span * span, second_span * span - span) + token
        low = jnp.zeros_like(place)
        for bound in bounds:
            low = jnp.maximum(low, jnp.where(place >= bound, bound, 0))
        at = pl.ds(pl.multiple_of(base, tile), tile)
        row_hi[at] = place
        row_lo[at] = low
        m_s[at] = jnp.full((tile, hd), masked_low, jnp.float32)
        for total in (l_s, wu_s, wd_s, wdu_s, acc_s):
            total[at] = jnp.zeros((tile, hd), jnp.float32)
        return carry

    lax.fori_loop(0, tiles, row_values, 0)
    q_in.wait()
    do_in.wait()

    def chunk_rows(zb, which):
        return kv[zb, :, which].reshape(chunk, hd)

    def forward_chunk(i, zb):
        key_rows, value_rows = chunk_rows(zb, 0), chunk_rows(zb, 1)
        lane = lax.broadcasted_iota(jnp.int32, (group, tok), 1)
        places = []
        for b in range(NX):
            owner = zb * NX + b
            lower = span_ref[owner * 2] * span
            upper = span_ref[owner * 2 + 1] * span - span
            place = jnp.where(lane < span, lower, upper) + lane
            places.append(
                jnp.broadcast_to(place[None], (tile // group, group, tok)).reshape(tile, tok)
            )
        factor = per_row(factor8)
        for r in range(tiles):
            at = slice(r * tile, (r + 1) * tile)
            raw = nt_dot(q_s[at], key_rows)
            low, high = row_lo[at], row_hi[at]
            scores = []
            for b in range(NX):
                visible = (places[b] >= low) & (places[b] <= high)
                score = jnp.where(visible, raw[:, b * tok : (b + 1) * tok] * factor, masked_low)
                s_s[i, at, b * tok : (b + 1) * tok] = score
                scores.append(score)
            peak = jnp.maximum(
                jnp.maximum(scores[0], scores[1]), jnp.maximum(scores[2], scores[3])
            )
            old = m_s[at]
            new = jnp.maximum(old, jnp.max(peak, axis=1, keepdims=True))
            m_s[at] = new
            shift = new - old
            alpha = jnp.exp(old - new)
            d_prob = nt_dot(do_s[at], value_rows)
            w_sum, wu_sum, wd_sum, wdu_sum = [jnp.zeros((tile, tok), jnp.float32)] * 4
            for b in range(NX):
                cols = slice(b * tok, (b + 1) * tok)
                below = scores[b] - new
                weight = jnp.exp(below)
                d_scaled = d_prob[:, cols] * factor
                p_s[at, cols] = weight.astype(jnp.bfloat16)
                dp_s[i, at, cols] = d_scaled
                weighted = weight * d_scaled
                w_sum, wu_sum = w_sum + weight, wu_sum + weight * below
                wd_sum, wdu_sum = wd_sum + weighted, wdu_sum + weighted * below
            w_old, wd_old = l_s[at], wd_s[at]
            wu_s[at] = alpha * (wu_s[at] - shift * w_old) + wu_sum
            wdu_s[at] = alpha * (wdu_s[at] - shift * wd_old) + wdu_sum
            l_s[at] = alpha * w_old + w_sum
            wd_s[at] = alpha * wd_old + wd_sum
            acc_s[at] = acc_s[at] * alpha
        acc_s[...] = acc_s[...] + nn_dot(p_s[...], value_rows)

    def gather_step(i, carry):
        for e in range(1, nz // 2 + 1):

            @pl.when(i == 2 * e - 1)
            def _():
                line_step(e)

        @pl.when((i > 0) & (i < nz))
        def _():
            x_sends(row(i))

        @pl.when((i >= X_LAG) & (i < nz + X_LAG))
        def _():
            relays(row(i - X_LAG))

        @pl.when(i >= 2 * X_LAG)
        def _():
            zb = row(i - 2 * X_LAG)
            row_waits(zb)
            forward_chunk(i - 2 * X_LAG, zb)

        return carry

    lax.fori_loop(0, nz + 2 * X_LAG, gather_step, 0)

    def finish_rows(r, hs_total):
        at = pl.ds(pl.multiple_of(r * tile, tile), tile)
        weights = l_s[at]
        total = jnp.sum(weights, axis=1, keepdims=True)
        log_total = jnp.log(total)
        out_rows = (acc_s[at] / total).astype(jnp.bfloat16)
        out_s[at] = out_rows
        m_s[at] = m_s[at] + log_total
        product = do_s[at].astype(jnp.float32) * out_rows.astype(jnp.float32)
        delta = jnp.sum(product, axis=1, keepdims=True) * per_row(factor8)
        terms = wdu_s[at] - delta * wu_s[at] - log_total * (wd_s[at] - delta * weights)
        l_s[at] = delta
        acc_s[at] = jnp.zeros((tile, hd), jnp.float32)
        return hs_total + jnp.sum((terms / total).reshape(tile // group, group, hd), axis=0)

    no_terms = jnp.zeros((group, hd), jnp.float32)
    h_own[...] = lax.fori_loop(0, tiles, finish_rows, no_terms)
    out_copy = pltpu.make_async_copy(out_s, out_hbm, in_sem.at[0])
    out_copy.start()

    def kv_share(t):
        return remote(h_own, h_kv.at[ki], h_send.at[0, t], hk_recv.at[ki], kv_dev(t))

    def plane_share(t):
        slot = core * NX + x
        return remote(h_kv, h_plane.at[slot], h_send.at[1, t], hp_recv.at[slot], plane_dev(t))

    def line_share():
        return remote(h_own_all, h_line.at[z], h_send.at[2, 0], hl_recv.at[z], line_dev(gate))

    def across_share():
        return remote(h_gate, h_hi.at[hi], h_send.at[3, 0], hh_recv.at[hi], across)

    def all_share(zz):
        return remote(h_all, h_all, h_send.at[4, zz], ha_recv.at[0], line_dev(zz))

    def arrived(buffer, sem):
        remote(buffer, buffer, sem, sem, right).wait_recv()

    for t in range(1, nk):
        kv_share(t).start()

    def share_plane():
        h_kv[ki] = h_own[...]
        for t in range(1, nk):
            slot = lax.rem(ki + t, nk)
            arrived(h_kv.at[slot], hk_recv.at[slot])
        for t in range(1, NX * cores):
            plane_share(t).start()

    def share_line():
        h_plane[core * NX + x] = h_kv[...]
        for t in range(1, NX * cores):
            slot = lax.rem(core + t // NX, cores) * NX + lax.rem(x + t % NX, NX)
            arrived(h_plane.at[slot], hp_recv.at[slot])
        total = h_plane[0]
        for t in range(1, NX * cores):
            total = total + h_plane[t]
        h_own_all[...] = total

        @pl.when(jnp.logical_not(at_gate))
        def _():
            line_share().start()

    def line_total():
        h_line[z] = h_own_all[...]

        def more(j, total):
            zz = lax.rem(gate + j, nz)
            arrived(h_line.at[zz], hl_recv.at[zz])
            return total

        lax.fori_loop(1, nz, more, 0)
        total = h_line[0]
        for zz in range(1, nz):
            total = total + h_line[zz]
        h_gate[...] = total

    def share_across():
        line_total()
        if nd > cores:
            across_share().start()

    def share_all():
        if nd > cores:
            arrived(h_hi.at[1 - hi], hh_recv.at[1 - hi])
            h_hi[hi] = h_gate[...]
            h_all[...] = h_hi[0] + h_hi[1]
        else:
            h_all[...] = h_gate[...]
        for j in range(1, nz):
            all_share(lax.rem(gate + j, nz)).start()

    for r in range(tiles):
        at = slice(r * tile, (r + 1) * tile)
        qt_s[:, at] = q_s[at].astype(jnp.float32).T.astype(jnp.bfloat16)
        dot_s[:, at] = do_s[at].astype(jnp.float32).T.astype(jnp.bfloat16)

    def a_copy(j, side):
        return remote(
            part.at[j, xo, side],
            rxa.at[j, side],
            a_send.at[j, side],
            a_recv.at[j, side],
            left if side == 0 else right,
        )

    def c_copy(j, side, piece):
        return remote(
            part.at[j, xl if side == 0 else xr, piece],
            rxc.at[j, side, piece],
            c_send.at[j, side, piece],
            c_recv.at[j, side, piece],
            left if side == 0 else right,
        )

    def line_sum(j, zb, side):
        return remote(
            part.at[j, x], rz.at[side, zb], z_send.at[side, zb], z_recv.at[side, zb],
            up if side == 0 else down,
        )

    def mate_sum(j, zb):
        return remote(part.at[j, x], rz.at[2, zb], z_send.at[2, zb], z_recv.at[2, zb], mate)

    def add_bf(a, b):
        return (a.astype(jnp.float32) + b.astype(jnp.float32)).astype(jnp.bfloat16)

    def neighbour_sums(j):
        a_copy(j, 0).wait_recv()
        part[j, xl, 0] = add_bf(part[j, xl, 0], rxa[j, 0])
        c_copy(j, 0, 0).start()
        a_copy(j, 1).wait_recv()
        part[j, xr, 1] = add_bf(part[j, xr, 1], rxa[j, 1])
        c_copy(j, 1, 1).start()

    def column_sums(j):
        for side in range(2):
            for piece in range(2):
                c_copy(j, side, piece).wait_recv()
        total = part[j, x].astype(jnp.float32) + rxc[j, 0].astype(jnp.float32)
        total = total + rxc[j, 1].astype(jnp.float32)
        part[j, x] = total.astype(jnp.bfloat16)

    def to_mate(s):
        def send(target):
            mate_sum(2 * xor_index(pair, target, nz // 2) + 1, zp + 2 * (target - pair)).start()

        if s == 0:
            send(pair)
        else:

            @pl.when(pair + s < nz // 2)
            def _():
                send(pair + s)

            @pl.when(pair >= s)
            def _():
                send(pair - s)

    def along_line(s):
        @pl.when(pair + s < nz // 2)
        def _():
            zb = z + 2 * s
            at = 2 * xor_index(pair, pair + s, nz // 2)
            mate_sum(at, zb).wait_recv()
            part[at, x] = add_bf(part[at, x], rz[2, zb])

            @pl.when(pair > 0)
            def _():
                line_sum(at, zb, 0).wait_recv()
                part[at, x] = add_bf(part[at, x], rz[0, zb])

            line_sum(at, zb, 0).start()

        @pl.when(pair >= s)
        def _():
            zb = z - 2 * s
            at = 2 * xor_index(pair, pair - s, nz // 2)
            mate_sum(at, zb).wait_recv()
            part[at, x] = add_bf(part[at, x], rz[2, zb])

            @pl.when(pair < nz // 2 - 1)
            def _():
                line_sum(at, zb, 1).wait_recv()
                part[at, x] = add_bf(part[at, x], rz[1, zb])

            line_sum(at, zb, 1).start()


    def backward_chunk(i):
        key_rows = chunk_rows(row(i), 0)
        for r in range(tiles):
            at = slice(r * tile, (r + 1) * tile)
            norm, delta = m_s[at], l_s[at]
            for b in range(NX):
                cols = slice(b * tok, (b + 1) * tok)
                prob = jnp.exp(s_s[i, at, cols] - norm)
                d_score = prob * (dp_s[i, at, cols] - delta)
                p_s[at, cols] = prob.astype(jnp.bfloat16)
                ds_s[at, cols] = d_score.astype(jnp.bfloat16)
            acc_s[at] = acc_s[at] + nn_dot(ds_s[at], key_rows)
        d_key = nn_dot(qt_s[...], ds_s[...])
        d_value = nn_dot(dot_s[...], p_s[...])
        for b in range(NX):
            cols = slice(b * tok, (b + 1) * tok)
            part[i, b, 0] = d_key[:, cols].astype(jnp.bfloat16)
            part[i, b, 1] = d_value[:, cols].astype(jnp.bfloat16)

    def scatter_step(k, carry):
        @pl.when(k < nz)
        def _():
            j = nz - 1 - k
            backward_chunk(j)
            a_copy(j, 0).start()
            a_copy(j, 1).start()
            c_copy(j, 0, 1).start()
            c_copy(j, 1, 0).start()

        @pl.when(k == nz - 1)
        def _():
            for r in range(tiles):
                at = slice(r * tile, (r + 1) * tile)
                dq_s[at] = acc_s[at].astype(jnp.bfloat16)
            dq_copy.start()

        @pl.when((k >= X_LAG) & (k < nz + X_LAG))
        def _():
            neighbour_sums(nz - 1 - k + X_LAG)

        @pl.when(k >= 2 * X_LAG)
        def _():
            j = nz - 1 - k + 2 * X_LAG
            column_sums(j)

        for f in range(nz // 2):

            @pl.when(k == 2 * X_LAG + 2 * f)
            def _():
                if f > 0:
                    along_line(nz // 2 - f)
                to_mate(nz // 2 - 1 - f)

        @pl.when(k == 1)
        def _():
            share_plane()

        @pl.when(k == 4)
        def _():
            share_line()

        @pl.when((k == nz) & at_gate)
        def _():
            share_across()

        @pl.when((k == nz + 2) & at_gate)
        def _():
            share_all()

        return carry

    dq_copy = pltpu.make_async_copy(dq_s, dq_hbm, in_sem.at[1])
    lax.fori_loop(0, nz + 2 * X_LAG, scatter_step, 0)

    total = part[0, x].astype(jnp.float32)
    mate_sum(0, z).wait_recv()
    rz_own = rz[2, z].astype(jnp.float32)
    part[0, x] = (total + rz_own).astype(jnp.bfloat16)

    @pl.when(pair > 0)
    def _():
        line_sum(0, z, 0).wait_recv()
        part[0, x] = add_bf(part[0, x], rz[0, z])

    @pl.when(pair < nz // 2 - 1)
    def _():
        line_sum(0, z, 1).wait_recv()
        part[0, x] = add_bf(part[0, x], rz[1, z])

    dk_ref[...] = part[0, x, 0].astype(jnp.float32).T.astype(jnp.bfloat16)
    dv_ref[...] = part[0, x, 1].astype(jnp.float32).T.astype(jnp.bfloat16)

    @pl.when(jnp.logical_not(at_gate))
    def _():
        arrived(h_all, ha_recv.at[0])

    for kk in range(nk):
        hs_ref[kk * group : (kk + 1) * group] = h_all[kk]

    for t in range(1, nk):
        kv_share(t).wait_send()
    for t in range(1, NX * cores):
        plane_share(t).wait_send()

    @pl.when(at_gate)
    def _():
        if nd > cores:
            across_share().wait_send()
        for j in range(1, nz):
            all_share(lax.rem(gate + j, nz)).wait_send()

    @pl.when(jnp.logical_not(at_gate))
    def _():
        line_share().wait_send()

    def drain(j, carry):
        for side in range(2):
            x_copy(j, x, side).wait_send()
            relay_copy(j, xl, side).wait_send()
            a_copy(j, side).wait_send()
            for piece in range(2):
                c_copy(j, side, piece).wait_send()
        same = lax.rem(z + j, 2) == 0

        @pl.when(same)
        def _():
            mate_copy(j).wait_send()

            @pl.when((j <= z) & (z < nz - 2))
            def _():
                line_copy(j, 0).wait_send()

            @pl.when((j >= z) & (z >= 2))
            def _():
                line_copy(j, 1).wait_send()

            @pl.when(j > z)
            def _():
                line_sum(0, j, 0).wait_send()

            @pl.when(j < z)
            def _():
                line_sum(0, j, 1).wait_send()

        @pl.when(jnp.logical_not(same))
        def _():
            mate_sum(0, j).wait_send()

        return carry

    lax.fori_loop(0, nz, drain, 0)
    out_copy.wait()
    dq_copy.wait()


def results(out_in, dq_in, dk_in, dv_in, hs_in, scale_in, out, dq, dk, dv, d_scale, buffers, sem):
    pairs = ((out_in, out), (dq_in, dq), (dk_in, dk), (dv_in, dv))
    rows = [pair[0].shape[0] for pair in pairs]
    views = [buffers.at[pl.ds(sum(rows[:i]), rows[i])] for i in range(4)]
    loads = [pltpu.make_async_copy(pairs[i][0], views[i], sem.at[0, i]) for i in range(4)]
    stores = [pltpu.make_async_copy(views[i], pairs[i][1], sem.at[1, i]) for i in range(4)]
    for load in loads:
        load.start()
    totals = jnp.sum(hs_in[...].T, axis=0, keepdims=True)
    scales = scale_in[...]
    d_scale[...] = totals * math.sqrt(out_in.shape[1]) / (scales * scales)
    for load, store in zip(loads, stores):
        load.wait()
        store.start()
    for store in stores:
        store.wait()


def local(queries, keys, values, d_out, head_scale, doc_lengths, span_order):
    _, tok, group, hd = queries.shape
    nz = lax.axis_size("ctx") // NX
    nk, nd = lax.axis_size("kvh"), lax.axis_size("dp")
    rows, chunk = tok * group, NX * tok
    bf, f32, i32 = jnp.bfloat16, jnp.float32, jnp.int32
    any_spec = pl.BlockSpec(memory_space=pl.ANY)
    vmem_spec = pl.BlockSpec(memory_space=pltpu.VMEM)
    smem_spec = pl.BlockSpec(memory_space=pltpu.SMEM)
    dma = pltpu.SemaphoreType.DMA
    out, dq, dk, dv, hs = pl.pallas_call(
        functools.partial(kernel, group, tok, hd, doc_lengths.shape[1], nk, nd),
        out_shape=(
            jax.ShapeDtypeStruct((rows, hd), bf),
            jax.ShapeDtypeStruct((rows, hd), bf),
            jax.ShapeDtypeStruct((tok, hd), bf),
            jax.ShapeDtypeStruct((tok, hd), bf),
            jax.ShapeDtypeStruct((nk * group, tok), f32),
        ),
        in_specs=[any_spec] * 4 + [smem_spec] * 3,
        out_specs=(any_spec, any_spec, vmem_spec, vmem_spec, vmem_spec),
        scratch_shapes=[
            pltpu.VMEM((rows, hd), bf),
            pltpu.VMEM((rows, hd), bf),
            pltpu.VMEM((hd, rows), bf),
            pltpu.VMEM((hd, rows), bf),
            pltpu.VMEM((nz, NX, 2, tok, hd), bf),
            pltpu.VMEM((nz, rows, chunk), f32),
            pltpu.VMEM((nz, rows, chunk), f32),
            pltpu.VMEM((rows, hd), i32),
            pltpu.VMEM((rows, hd), i32),
            pltpu.VMEM((rows, hd), f32),
            pltpu.VMEM((rows, hd), f32),
            pltpu.VMEM((rows, hd), f32),
            pltpu.VMEM((rows, hd), f32),
            pltpu.VMEM((rows, hd), f32),
            pltpu.VMEM((rows, hd), f32),
            pltpu.VMEM((rows, hd), bf),
            pltpu.VMEM((rows, hd), bf),
            pltpu.VMEM((rows, chunk), bf),
            pltpu.VMEM((rows, chunk), bf),
            pltpu.VMEM((nz, NX, 2, hd, tok), bf),
            pltpu.VMEM((nz, 2, hd, tok), bf),
            pltpu.VMEM((nz, 2, 2, hd, tok), bf),
            pltpu.VMEM((3, nz, 2, hd, tok), bf),
            pltpu.VMEM((group, hd), f32),
            pltpu.VMEM((nk, group, hd), f32),
            pltpu.VMEM((2 * NX, nk, group, hd), f32),
            pltpu.VMEM((nk, group, hd), f32),
            pltpu.VMEM((nz, nk, group, hd), f32),
            pltpu.VMEM((nk, group, hd), f32),
            pltpu.VMEM((2, nk, group, hd), f32),
            pltpu.VMEM((nk, group, hd), f32),
            dma((4,)),
            dma((nz, NX, 2)),
            dma((3, nz)),
            dma((2, nz)),
            dma((2, nz)),
            dma((nz, 2)),
            dma((nz, 2)),
            dma((nz, 2, 2)),
            dma((nz, 2, 2)),
            dma((3, nz)),
            dma((3, nz)),
            dma((5, 2 * NX)),
            dma((nk,)),
            dma((2 * NX,)),
            dma((nz,)),
            dma((2,)),
            dma((1,)),
        ],
        compiler_params=pltpu.CompilerParams(
            collective_id=0, has_side_effects=True, vmem_limit_bytes=60 * 1024 * 1024
        ),
    )(
        queries.reshape(rows, hd),
        keys.reshape(tok, hd),
        values.reshape(tok, hd),
        d_out.reshape(rows, hd),
        head_scale,
        doc_lengths,
        span_order,
    )
    out, dq, dk, dv, d_head_scale = pl.pallas_call(
        results,
        out_shape=(
            jax.ShapeDtypeStruct((rows, hd), bf),
            jax.ShapeDtypeStruct((rows, hd), bf),
            jax.ShapeDtypeStruct((tok, hd), bf),
            jax.ShapeDtypeStruct((tok, hd), bf),
            jax.ShapeDtypeStruct((1, nk * group), f32),
        ),
        in_specs=[any_spec] * 4 + [vmem_spec] * 2,
        out_specs=(any_spec, any_spec, any_spec, any_spec, vmem_spec),
        scratch_shapes=[pltpu.VMEM((2 * (rows + tok), hd), bf), dma((2, 4))],
    )(out, dq, dk, dv, hs, head_scale.reshape(1, nk * group))
    return (
        out.reshape(queries.shape),
        dq.reshape(queries.shape),
        dk.reshape(keys.shape),
        dv.reshape(values.shape),
        d_head_scale.reshape(head_scale.shape),
    )


def solution(mesh):
    return jax.shard_map(
        local,
        mesh=mesh,
        in_specs=(
            P("dp", "ctx", "kvh", None),
            P("dp", "ctx", "kvh", None),
            P("dp", "ctx", "kvh", None),
            P("dp", "ctx", "kvh", None),
            P(),
            P("dp", None),
            P(),
        ),
        out_specs=(
            P("dp", "ctx", "kvh", None),
            P("dp", "ctx", "kvh", None),
            P("dp", "ctx", "kvh", None),
            P("dp", "ctx", "kvh", None),
            P(),
        ),
        check_vma=False,
    )
```

```python
import functools
import math

import jax
import jax.numpy as jnp
from jax import lax
from jax.experimental import pallas as pl
from jax.experimental.pallas import tpu as pltpu
from jax.sharding import PartitionSpec as P

MESH = pl.DeviceIdType.MESH
masked_low = -1e30
hidden = -16384.0
NX = 4
X_LAG = 2
RELAY_LAG = 2
ROW_LAG = 4


def nt_dot(a, b):
    return lax.dot_general(a, b, (((1,), (1,)), ((), ())), preferred_element_type=jnp.float32)


def nn_dot(a, b):
    return lax.dot_general(a, b, (((1,), (0,)), ((), ())), preferred_element_type=jnp.float32)


def xor_index(a, b, count):
    total, bit = 0, 1
    while bit < count:
        total = total + (lax.rem(lax.div(a, bit) + lax.div(b, bit), 2)) * bit
        bit *= 2
    return total


def kernel(
    group, tok, hd, docs, nk, nd,
    q_hbm, k_hbm, v_hbm, do_hbm, scale_ref, docs_ref, span_ref,
    out_hbm, dq_hbm, dk_ref, dv_ref, hs_ref,
    q_s, qf_s, do_s, qt_s, dot_s, kv, s_s, dp_s, row_lo, row_hi, m_s, l_s, wu_s, wd_s, wdu_s, acc_s,
    out_s, dq_s, p_s, ds_s, part, rxa, rxc, rz, h_own, h_kv, h_plane, h_own_all, h_line, h_gate, h_hi, h_all,
    in_sem, g_recv, gz_send, gx_send, gr_send, a_send, a_recv,
    c_send, c_recv, z_send, z_recv,
    h_send, hk_recv, hp_recv, hl_recv, hh_recv, ha_recv,
):
    nz = lax.axis_size("ctx") // NX
    rows = group * tok
    chunk = NX * tok
    span = tok // 2
    tile = min(512, rows)
    tiles = rows // tile
    me = lax.axis_index("ctx")
    ki, di = lax.axis_index("kvh"), lax.axis_index("dp")
    z, x = lax.div(me, NX), lax.rem(me, NX)
    pair = lax.div(z, 2)
    zp = z + 1 - 2 * lax.rem(z, 2)
    xr, xl, xo = lax.rem(x + 1, NX), lax.rem(x + 3, NX), lax.rem(x + 2, NX)

    def row(j):
        return xor_index(z, jnp.int32(j), nz)

    def x_dev(shift):
        return {"ctx": z * NX + lax.rem(x + shift, NX)}

    right, left = x_dev(1), x_dev(3)
    mate = {"ctx": zp * NX + x}
    up = {"ctx": lax.rem(z + 2, nz) * NX + x}
    down = {"ctx": lax.rem(z + nz - 2, nz) * NX + x}

    cores = min(2, nd)
    core, hi = lax.rem(di, cores), lax.div(di, cores)
    gate = (nz - 1) * (1 - hi)
    at_gate = z == gate

    def kv_dev(t):
        return {"kvh": lax.rem(ki + t, nk)}

    def plane_dev(t):
        to_core = lax.rem(core + t // NX, cores)
        return {"ctx": z * NX + lax.rem(x + t % NX, NX), "dp": hi * cores + to_core}

    def line_dev(zz):
        return {"ctx": zz * NX + x}

    across = {"ctx": (nz - 1) * hi * NX + x, "dp": lax.rem(di + cores, nd)}

    k_in = pltpu.make_async_copy(k_hbm, kv.at[z, x, 0], in_sem.at[0])
    v_in = pltpu.make_async_copy(v_hbm, kv.at[z, x, 1], in_sem.at[1])
    q_in = pltpu.make_async_copy(q_hbm, q_s, in_sem.at[2])
    do_in = pltpu.make_async_copy(do_hbm, do_s, in_sem.at[3])
    for load in (k_in, v_in, q_in, do_in):
        load.start()

    barrier = pltpu.get_barrier_semaphore()
    partners = [mate] + [kv_dev(t) for t in range(1, nk)]
    partners = partners + [plane_dev(t) for t in range(1, NX * cores)]

    def greet(partner):
        pl.semaphore_signal(barrier, inc=1, device_id=partner, device_id_type=MESH)

    for partner in partners:
        greet(partner)

    @pl.when(z < nz - 2)
    def _():
        greet(up)

    @pl.when(z >= 2)
    def _():
        greet(down)

    inner = jnp.where((z >= 2) & (z < nz - 2), 1, 0)
    if nd > cores:

        @pl.when(at_gate)
        def _():
            greet(across)

        inner = inner + jnp.where(at_gate, 1, 0)
    pl.semaphore_wait(barrier, len(partners) + 1 + inner)

    def remote(src, dst, send_sem, recv_sem, device):
        return pltpu.make_async_remote_copy(
            src_ref=src,
            dst_ref=dst,
            send_sem=send_sem,
            recv_sem=recv_sem,
            device_id=device,
            device_id_type=MESH,
        )

    def piece_copy(zb, bx, piece, send_sem, device):
        at = (zb, bx, piece)
        return remote(kv.at[at], kv.at[at], send_sem, g_recv.at[at], device)

    def line_copy(origin, side, piece):
        sem = gz_send.at[side, origin, piece]
        return piece_copy(origin, x, piece, sem, up if side == 0 else down)

    def mate_copy(origin, piece):
        return piece_copy(origin, x, piece, gz_send.at[2, origin, piece], mate)

    def x_copy(zb, bx, side, piece):
        sem = gx_send.at[side, zb, piece]
        return piece_copy(zb, bx, piece, sem, right if side == 0 else left)

    def relay_copy(zb, bx, side):
        at = (zb, bx, side)
        return remote(
            kv.at[at], kv.at[at], gr_send.at[side, zb], g_recv.at[at], right if side == 0 else left
        )

    def x_sends(zb):
        for side, piece in ((0, 0), (1, 1), (0, 1), (1, 0)):
            x_copy(zb, x, side, piece).start()

    def relays(zb):
        x_copy(zb, xl, 0, 0).wait_recv()
        relay_copy(zb, xl, 0).start()
        x_copy(zb, xr, 1, 1).wait_recv()
        relay_copy(zb, xr, 1).start()

    def row_waits(zb):
        x_copy(zb, xl, 0, 1).wait_recv()
        x_copy(zb, xr, 1, 0).wait_recv()
        relay_copy(zb, xo, 0).wait_recv()
        relay_copy(zb, xo, 1).wait_recv()

    def forward_line(origin, side, piece):
        @pl.when((z < nz - 2) if side == 0 else (z >= 2))
        def _():
            line_copy(origin, side, piece).start()

    def line_step(e):
        if e < nz // 2:
            for piece in range(2):

                @pl.when(z >= 2 * e)
                def _():
                    line_copy(z - 2 * e, 0, piece).wait_recv()
                    forward_line(z - 2 * e, 0, piece)
                    mate_copy(z - 2 * e, piece).start()

                @pl.when(z + 2 * e < nz)
                def _():
                    line_copy(z + 2 * e, 1, piece).wait_recv()
                    forward_line(z + 2 * e, 1, piece)
                    mate_copy(z + 2 * e, piece).start()

        for piece in range(2):
            if e == 1:
                mate_copy(zp, piece).wait_recv()
            else:

                @pl.when(zp >= 2 * (e - 1))
                def _():
                    mate_copy(zp - 2 * (e - 1), piece).wait_recv()

                @pl.when(zp + 2 * (e - 1) < nz)
                def _():
                    mate_copy(zp + 2 * (e - 1), piece).wait_recv()

    k_in.wait()
    forward_line(z, 0, 0)
    forward_line(z, 1, 0)
    v_in.wait()
    forward_line(z, 0, 1)
    forward_line(z, 1, 1)
    mate_copy(z, 0).start()
    mate_copy(z, 1).start()
    x_sends(z)

    head0 = ki * group
    sub = lax.broadcasted_iota(jnp.int32, (group, hd), 0)
    scale8 = jnp.zeros((group, hd), jnp.float32)
    for h in range(group):
        scale8 = jnp.where(sub == h, scale_ref[head0 + h], scale8)
    factor8 = scale8 * (1.0 / math.sqrt(hd))

    def per_row(tile8):
        return jnp.broadcast_to(tile8[None], (tile // group, group, hd)).reshape(tile, hd)

    bounds = []
    running = jnp.int32(0)
    for d in range(docs):
        running = running + docs_ref[0, d]
        bounds.append(running)
    first_span, second_span = span_ref[2 * me], span_ref[2 * me + 1]

    blocks = span_ref.shape[0]
    lane1 = lax.broadcasted_iota(jnp.int32, (1, hd), 1)
    doc_low = jnp.full((1, hd), 1 << 30, jnp.int32)
    doc_high = jnp.zeros((1, hd), jnp.int32)
    for d in range(docs):
        doc_low = jnp.where(lane1 == blocks + d, bounds[d - 1] if d else 0, doc_low)
        doc_high = jnp.where(lane1 == blocks + d, bounds[d], doc_high)
    doc_lane = (lane1 >= blocks) & (lane1 < blocks + docs)

    def row_values(r, carry):
        base = r * tile
        token = (lax.broadcasted_iota(jnp.int32, (tile, hd), 0) + base) // group
        place = jnp.where(token < span, first_span * span, second_span * span - span) + token
        low = jnp.zeros_like(place)
        for bound in bounds:
            low = jnp.maximum(low, jnp.where(place >= bound, bound, 0))
        at = pl.ds(pl.multiple_of(base, tile), tile)
        row_hi[at] = place
        lane = lax.broadcasted_iota(jnp.int32, (tile, hd), 1)
        later = (lane < blocks) & (lane * span > place)
        other = doc_lane & ((place < doc_low) | (place >= doc_high))
        qf_s[at] = jnp.where(later | other, hidden, 0.0).astype(jnp.bfloat16)
        row_lo[at] = low
        m_s[at] = jnp.full((tile, hd), masked_low, jnp.float32)
        for total in (l_s, wu_s, wd_s, wdu_s, acc_s):
            total[at] = jnp.zeros((tile, hd), jnp.float32)
        return carry

    lax.fori_loop(0, tiles, row_values, 0)
    q_in.wait()
    do_in.wait()

    def chunk_rows(zb, which):
        return kv[zb, :, which].reshape(chunk, hd)

    def forward_chunk(i, zb, own):
        key_rows, value_rows = chunk_rows(zb, 0), chunk_rows(zb, 1)
        lane = lax.broadcasted_iota(jnp.int32, (group, tok), 1)
        key_lane = lax.broadcasted_iota(jnp.int32, (tok, hd), 1)
        key_row = lax.broadcasted_iota(jnp.int32, (tok, hd), 0)
        places, features = [], []
        for b in range(NX):
            owner = zb * NX + b
            lower, upper = span_ref[owner * 2], span_ref[owner * 2 + 1]
            block = jnp.where(key_row < span, lower, upper)
            key_place = block * span + jnp.where(key_row < span, key_row, key_row - span)
            marked = (key_lane == block) | ((key_place >= doc_low) & (key_place < doc_high))
            features.append(jnp.where(marked, 1.0, 0.0).astype(jnp.bfloat16))
            place = jnp.where(lane < span, lower * span, upper * span - span) + lane
            places.append(
                jnp.broadcast_to(place[None], (tile // group, group, tok)).reshape(tile, tok)
            )
        key_rows = jnp.concatenate([key_rows, jnp.concatenate(features, axis=0)], axis=1)
        factor = per_row(factor8)
        for r in range(tiles):
            at = slice(r * tile, (r + 1) * tile)
            raw = nt_dot(jnp.concatenate([q_s[at], qf_s[at]], axis=1), key_rows)
            low, high = row_lo[at], row_hi[at]
            scores = []
            for b in range(NX):
                score = raw[:, b * tok : (b + 1) * tok] * factor
                if own:
                    visible = (places[b] >= low) & (places[b] <= high)
                    score = jnp.where(visible, score, masked_low)
                s_s[i, at, b * tok : (b + 1) * tok] = score
                scores.append(score)
            peak = jnp.maximum(
                jnp.maximum(scores[0], scores[1]), jnp.maximum(scores[2], scores[3])
            )
            old = m_s[at]
            new = jnp.maximum(old, jnp.max(peak, axis=1, keepdims=True))
            m_s[at] = new
            shift = new - old
            alpha = jnp.exp(old - new)
            d_prob = nt_dot(do_s[at], value_rows)
            w_sum, wu_sum, wd_sum, wdu_sum = [jnp.zeros((tile, tok), jnp.float32)] * 4
            for b in range(NX):
                cols = slice(b * tok, (b + 1) * tok)
                below = scores[b] - new
                weight = jnp.exp(below)
                d_here = d_prob[:, cols]
                p_s[at, cols] = weight.astype(jnp.bfloat16)
                dp_s[i, at, cols] = d_here
                weighted = weight * d_here
                w_sum, wu_sum = w_sum + weight, wu_sum + weight * below
                wd_sum, wdu_sum = wd_sum + weighted, wdu_sum + weighted * below
            w_old, wd_old = l_s[at], wd_s[at]
            wu_s[at] = alpha * (wu_s[at] - shift * w_old) + wu_sum
            wdu_s[at] = alpha * (wdu_s[at] - shift * wd_old) + wdu_sum
            l_s[at] = alpha * w_old + w_sum
            wd_s[at] = alpha * wd_old + wd_sum
            acc_s[at] = acc_s[at] * alpha
        acc_s[...] = acc_s[...] + nn_dot(p_s[...], value_rows)

    def gather_step(i, carry):
        @pl.when(i == 0)
        def _():
            for r in range(tiles):
                at = slice(r * tile, (r + 1) * tile)
                qt_s[:, at] = q_s[at].astype(jnp.float32).T.astype(jnp.bfloat16)
                dot_s[:, at] = do_s[at].astype(jnp.float32).T.astype(jnp.bfloat16)

        for e in range(1, nz // 2 + 1):

            @pl.when(i == 2 * e - 1)
            def _():
                line_step(e)

        @pl.when((i > 0) & (i < nz))
        def _():
            x_sends(row(i))

        @pl.when((i >= RELAY_LAG) & (i < nz + RELAY_LAG))
        def _():
            relays(row(i - RELAY_LAG))

        @pl.when(i >= ROW_LAG)
        def _():
            zb = row(i - ROW_LAG)
            row_waits(zb)

            @pl.when(i == ROW_LAG)
            def _():
                forward_chunk(0, zb, True)

            @pl.when(i > ROW_LAG)
            def _():
                forward_chunk(i - ROW_LAG, zb, False)

        return carry

    lax.fori_loop(0, nz + ROW_LAG, gather_step, 0)

    def finish_rows(r, hs_total):
        at = pl.ds(pl.multiple_of(r * tile, tile), tile)
        weights = l_s[at]
        total = jnp.sum(weights, axis=1, keepdims=True)
        log_total = jnp.log(total)
        out_rows = (acc_s[at] / total).astype(jnp.bfloat16)
        out_s[at] = out_rows
        m_s[at] = m_s[at] + log_total
        product = do_s[at].astype(jnp.float32) * out_rows.astype(jnp.float32)
        delta = jnp.sum(product, axis=1, keepdims=True)
        terms = wdu_s[at] - delta * wu_s[at] - log_total * (wd_s[at] - delta * weights)
        l_s[at] = jnp.broadcast_to(delta, (tile, hd))
        acc_s[at] = jnp.zeros((tile, hd), jnp.float32)
        return hs_total + jnp.sum((terms / total).reshape(tile // group, group, hd), axis=0)

    no_terms = jnp.zeros((group, hd), jnp.float32)
    h_own[...] = lax.fori_loop(0, tiles, finish_rows, no_terms)
    out_copy = pltpu.make_async_copy(out_s, out_hbm, in_sem.at[0])
    out_copy.start()

    def kv_share(t):
        return remote(h_own, h_kv.at[ki], h_send.at[0, t], hk_recv.at[ki], kv_dev(t))

    def plane_share(t):
        slot = core * NX + x
        return remote(h_kv, h_plane.at[slot], h_send.at[1, t], hp_recv.at[slot], plane_dev(t))

    def line_share():
        return remote(h_own_all, h_line.at[z], h_send.at[2, 0], hl_recv.at[z], line_dev(gate))

    def across_share():
        return remote(h_gate, h_hi.at[hi], h_send.at[3, 0], hh_recv.at[hi], across)

    def all_share(zz):
        return remote(h_all, h_all, h_send.at[4, zz], ha_recv.at[0], line_dev(zz))

    def arrived(buffer, sem):
        remote(buffer, buffer, sem, sem, right).wait_recv()

    for t in range(1, nk):
        kv_share(t).start()

    def share_plane():
        h_kv[ki] = h_own[...]
        for t in range(1, nk):
            slot = lax.rem(ki + t, nk)
            arrived(h_kv.at[slot], hk_recv.at[slot])
        for t in range(1, NX * cores):
            plane_share(t).start()

    def share_line():
        h_plane[core * NX + x] = h_kv[...]
        for t in range(1, NX * cores):
            slot = lax.rem(core + t // NX, cores) * NX + lax.rem(x + t % NX, NX)
            arrived(h_plane.at[slot], hp_recv.at[slot])
        total = h_plane[0]
        for t in range(1, NX * cores):
            total = total + h_plane[t]
        h_own_all[...] = total

        @pl.when(jnp.logical_not(at_gate))
        def _():
            line_share().start()

    def line_total():
        h_line[z] = h_own_all[...]

        def more(j, total):
            zz = lax.rem(gate + j, nz)
            arrived(h_line.at[zz], hl_recv.at[zz])
            return total

        lax.fori_loop(1, nz, more, 0)
        total = h_line[0]
        for zz in range(1, nz):
            total = total + h_line[zz]
        h_gate[...] = total

    def share_across():
        line_total()
        if nd > cores:
            across_share().start()

    def share_all():
        if nd > cores:
            arrived(h_hi.at[1 - hi], hh_recv.at[1 - hi])
            h_hi[hi] = h_gate[...]
            h_all[...] = h_hi[0] + h_hi[1]
        else:
            h_all[...] = h_gate[...]
        for j in range(1, nz):
            all_share(lax.rem(gate + j, nz)).start()


    def a_copy(j, side):
        return remote(
            part.at[j, xo, side],
            rxa.at[j, side],
            a_send.at[j, side],
            a_recv.at[j, side],
            left if side == 0 else right,
        )

    def c_copy(j, side, piece):
        return remote(
            part.at[j, xl if side == 0 else xr, piece],
            rxc.at[j, side, piece],
            c_send.at[j, side, piece],
            c_recv.at[j, side, piece],
            left if side == 0 else right,
        )

    def line_sum(j, zb, side, piece):
        return remote(
            part.at[j, x, piece],
            rz.at[side, zb, piece],
            z_send.at[side, zb, piece],
            z_recv.at[side, zb, piece],
            up if side == 0 else down,
        )

    def mate_sum(j, zb, piece):
        return remote(
            part.at[j, x, piece],
            rz.at[2, zb, piece],
            z_send.at[2, zb, piece],
            z_recv.at[2, zb, piece],
            mate,
        )

    def add_bf(a, b):
        return (a.astype(jnp.float32) + b.astype(jnp.float32)).astype(jnp.bfloat16)

    def neighbour_sums(j):
        a_copy(j, 0).wait_recv()
        part[j, xl, 0] = add_bf(part[j, xl, 0], rxa[j, 0])
        c_copy(j, 0, 0).start()
        a_copy(j, 1).wait_recv()
        part[j, xr, 1] = add_bf(part[j, xr, 1], rxa[j, 1])
        c_copy(j, 1, 1).start()

    def column_sums(j):
        for side in range(2):
            for piece in range(2):
                c_copy(j, side, piece).wait_recv()
        total = part[j, x].astype(jnp.float32) + rxc[j, 0].astype(jnp.float32)
        total = total + rxc[j, 1].astype(jnp.float32)
        part[j, x] = total.astype(jnp.bfloat16)

    def to_mate(s):
        def send(target):
            for piece in range(2):
                at = 2 * xor_index(pair, target, nz // 2) + 1
                mate_sum(at, zp + 2 * (target - pair), piece).start()

        if s == 0:
            send(pair)
        else:

            @pl.when(pair + s < nz // 2)
            def _():
                send(pair + s)

            @pl.when(pair >= s)
            def _():
                send(pair - s)

    def along_line(s):
        for piece in range(2):
            for side, far in ((0, s), (1, -s)):

                @pl.when((pair + s < nz // 2) if side == 0 else (pair >= s))
                def _():
                    zb = z + 2 * far
                    at = 2 * xor_index(pair, pair + far, nz // 2)
                    mate_sum(at, zb, piece).wait_recv()
                    part[at, x, piece] = add_bf(part[at, x, piece], rz[2, zb, piece])

                    @pl.when((pair > 0) if side == 0 else (pair < nz // 2 - 1))
                    def _():
                        line_sum(at, zb, side, piece).wait_recv()
                        part[at, x, piece] = add_bf(part[at, x, piece], rz[side, zb, piece])

                    line_sum(at, zb, side, piece).start()

    def backward_chunk(i):
        key_rows = chunk_rows(row(i), 0)
        factor = per_row(factor8)
        for r in range(tiles):
            at = slice(r * tile, (r + 1) * tile)
            norm, delta = m_s[at], l_s[at]
            for b in range(NX):
                cols = slice(b * tok, (b + 1) * tok)
                prob = jnp.exp(s_s[i, at, cols] - norm)
                d_score = prob * ((dp_s[i, at, cols] - delta) * factor)
                p_s[at, cols] = prob.astype(jnp.bfloat16)
                ds_s[at, cols] = d_score.astype(jnp.bfloat16)
            acc_s[at] = acc_s[at] + nn_dot(ds_s[at], key_rows)
        d_key = nn_dot(qt_s[...], ds_s[...])
        d_value = nn_dot(dot_s[...], p_s[...])
        for b in range(NX):
            cols = slice(b * tok, (b + 1) * tok)
            part[i, b, 0] = d_key[:, cols].astype(jnp.bfloat16)
            part[i, b, 1] = d_value[:, cols].astype(jnp.bfloat16)

    def scatter_step(k, carry):
        @pl.when(k < nz)
        def _():
            j = nz - 1 - k
            backward_chunk(j)
            a_copy(j, 0).start()
            a_copy(j, 1).start()
            c_copy(j, 0, 1).start()
            c_copy(j, 1, 0).start()

        @pl.when(k == nz - 1)
        def _():
            for r in range(tiles):
                at = slice(r * tile, (r + 1) * tile)
                dq_s[at] = acc_s[at].astype(jnp.bfloat16)
            dq_copy.start()

        @pl.when((k >= X_LAG) & (k < nz + X_LAG))
        def _():
            neighbour_sums(nz - 1 - k + X_LAG)

        @pl.when(k >= 2 * X_LAG)
        def _():
            j = nz - 1 - k + 2 * X_LAG
            column_sums(j)

        for f in range(nz // 2):

            @pl.when(k == 2 * X_LAG + 2 * f)
            def _():
                if f > 0:
                    along_line(nz // 2 - f)
                to_mate(nz // 2 - 1 - f)

        @pl.when(k == 1)
        def _():
            share_plane()

        @pl.when(k == 4)
        def _():
            share_line()

        @pl.when((k == nz) & at_gate)
        def _():
            share_across()

        @pl.when((k == nz + 2) & at_gate)
        def _():
            share_all()

        return carry

    dq_copy = pltpu.make_async_copy(dq_s, dq_hbm, in_sem.at[1])
    lax.fori_loop(0, nz + 2 * X_LAG, scatter_step, 0)

    for piece in range(2):
        mate_sum(0, z, piece).wait_recv()
    part[0, x] = add_bf(part[0, x], rz[2, z])

    @pl.when(pair > 0)
    def _():
        for piece in range(2):
            line_sum(0, z, 0, piece).wait_recv()
        part[0, x] = add_bf(part[0, x], rz[0, z])

    @pl.when(pair < nz // 2 - 1)
    def _():
        for piece in range(2):
            line_sum(0, z, 1, piece).wait_recv()
        part[0, x] = add_bf(part[0, x], rz[1, z])

    dk_ref[...] = part[0, x, 0].astype(jnp.float32).T.astype(jnp.bfloat16)
    dv_ref[...] = part[0, x, 1].astype(jnp.float32).T.astype(jnp.bfloat16)

    @pl.when(jnp.logical_not(at_gate))
    def _():
        arrived(h_all, ha_recv.at[0])

    for kk in range(nk):
        hs_ref[kk * group : (kk + 1) * group] = h_all[kk]

    for t in range(1, nk):
        kv_share(t).wait_send()
    for t in range(1, NX * cores):
        plane_share(t).wait_send()

    @pl.when(at_gate)
    def _():
        if nd > cores:
            across_share().wait_send()
        for j in range(1, nz):
            all_share(lax.rem(gate + j, nz)).wait_send()

    @pl.when(jnp.logical_not(at_gate))
    def _():
        line_share().wait_send()

    def drain(j, carry):
        for side in range(2):
            relay_copy(j, xl, side).wait_send()
            a_copy(j, side).wait_send()
            for piece in range(2):
                x_copy(j, x, side, piece).wait_send()
                c_copy(j, side, piece).wait_send()
        same = lax.rem(z + j, 2) == 0
        for piece in range(2):

            @pl.when(same)
            def _():
                mate_copy(j, piece).wait_send()

                @pl.when((j <= z) & (z < nz - 2))
                def _():
                    line_copy(j, 0, piece).wait_send()

                @pl.when((j >= z) & (z >= 2))
                def _():
                    line_copy(j, 1, piece).wait_send()

                @pl.when(j > z)
                def _():
                    line_sum(0, j, 0, piece).wait_send()

                @pl.when(j < z)
                def _():
                    line_sum(0, j, 1, piece).wait_send()

            @pl.when(jnp.logical_not(same))
            def _():
                mate_sum(0, j, piece).wait_send()

        return carry

    lax.fori_loop(0, nz, drain, 0)
    out_copy.wait()
    dq_copy.wait()


def results(out_in, dq_in, dk_in, dv_in, hs_in, scale_in, out, dq, dk, dv, d_scale, buffers, sem):
    pairs = ((out_in, out), (dq_in, dq), (dk_in, dk), (dv_in, dv))
    rows = [pair[0].shape[0] for pair in pairs]
    views = [buffers.at[pl.ds(sum(rows[:i]), rows[i])] for i in range(4)]
    loads = [pltpu.make_async_copy(pairs[i][0], views[i], sem.at[0, i]) for i in range(4)]
    stores = [pltpu.make_async_copy(views[i], pairs[i][1], sem.at[1, i]) for i in range(4)]
    for load in loads:
        load.start()
    totals = jnp.sum(hs_in[...].T, axis=0, keepdims=True)
    scales = scale_in[...]
    d_scale[...] = totals / scales
    for load, store in zip(loads, stores):
        load.wait()
        store.start()
    for store in stores:
        store.wait()


def local(queries, keys, values, d_out, head_scale, doc_lengths, span_order):
    _, tok, group, hd = queries.shape
    nz = lax.axis_size("ctx") // NX
    nk, nd = lax.axis_size("kvh"), lax.axis_size("dp")
    rows, chunk = tok * group, NX * tok
    bf, f32, i32 = jnp.bfloat16, jnp.float32, jnp.int32
    any_spec = pl.BlockSpec(memory_space=pl.ANY)
    vmem_spec = pl.BlockSpec(memory_space=pltpu.VMEM)
    smem_spec = pl.BlockSpec(memory_space=pltpu.SMEM)
    dma = pltpu.SemaphoreType.DMA
    out, dq, dk, dv, hs = pl.pallas_call(
        functools.partial(kernel, group, tok, hd, doc_lengths.shape[1], nk, nd),
        out_shape=(
            jax.ShapeDtypeStruct((rows, hd), bf),
            jax.ShapeDtypeStruct((rows, hd), bf),
            jax.ShapeDtypeStruct((tok, hd), bf),
            jax.ShapeDtypeStruct((tok, hd), bf),
            jax.ShapeDtypeStruct((nk * group, tok), f32),
        ),
        in_specs=[any_spec] * 4 + [smem_spec] * 3,
        out_specs=(any_spec, any_spec, vmem_spec, vmem_spec, vmem_spec),
        scratch_shapes=[
            pltpu.VMEM((rows, hd), bf),
            pltpu.VMEM((rows, hd), bf),
            pltpu.VMEM((rows, hd), bf),
            pltpu.VMEM((hd, rows), bf),
            pltpu.VMEM((hd, rows), bf),
            pltpu.VMEM((nz, NX, 2, tok, hd), bf),
            pltpu.VMEM((nz, rows, chunk), f32),
            pltpu.VMEM((nz, rows, chunk), f32),
            pltpu.VMEM((rows, hd), i32),
            pltpu.VMEM((rows, hd), i32),
            pltpu.VMEM((rows, hd), f32),
            pltpu.VMEM((rows, hd), f32),
            pltpu.VMEM((rows, hd), f32),
            pltpu.VMEM((rows, hd), f32),
            pltpu.VMEM((rows, hd), f32),
            pltpu.VMEM((rows, hd), f32),
            pltpu.VMEM((rows, hd), bf),
            pltpu.VMEM((rows, hd), bf),
            pltpu.VMEM((rows, chunk), bf),
            pltpu.VMEM((rows, chunk), bf),
            pltpu.VMEM((nz, NX, 2, hd, tok), bf),
            pltpu.VMEM((nz, 2, hd, tok), bf),
            pltpu.VMEM((nz, 2, 2, hd, tok), bf),
            pltpu.VMEM((3, nz, 2, hd, tok), bf),
            pltpu.VMEM((group, hd), f32),
            pltpu.VMEM((nk, group, hd), f32),
            pltpu.VMEM((2 * NX, nk, group, hd), f32),
            pltpu.VMEM((nk, group, hd), f32),
            pltpu.VMEM((nz, nk, group, hd), f32),
            pltpu.VMEM((nk, group, hd), f32),
            pltpu.VMEM((2, nk, group, hd), f32),
            pltpu.VMEM((nk, group, hd), f32),
            dma((4,)),
            dma((nz, NX, 2)),
            dma((3, nz, 2)),
            dma((2, nz, 2)),
            dma((2, nz)),
            dma((nz, 2)),
            dma((nz, 2)),
            dma((nz, 2, 2)),
            dma((nz, 2, 2)),
            dma((3, nz, 2)),
            dma((3, nz, 2)),
            dma((5, 2 * NX)),
            dma((nk,)),
            dma((2 * NX,)),
            dma((nz,)),
            dma((2,)),
            dma((1,)),
        ],
        compiler_params=pltpu.CompilerParams(
            collective_id=0, has_side_effects=True, vmem_limit_bytes=60 * 1024 * 1024
        ),
    )(
        queries.reshape(rows, hd),
        keys.reshape(tok, hd),
        values.reshape(tok, hd),
        d_out.reshape(rows, hd),
        head_scale,
        doc_lengths,
        span_order,
    )
    out, dq, dk, dv, d_head_scale = pl.pallas_call(
        results,
        out_shape=(
            jax.ShapeDtypeStruct((rows, hd), bf),
            jax.ShapeDtypeStruct((rows, hd), bf),
            jax.ShapeDtypeStruct((tok, hd), bf),
            jax.ShapeDtypeStruct((tok, hd), bf),
            jax.ShapeDtypeStruct((1, nk * group), f32),
        ),
        in_specs=[any_spec] * 4 + [vmem_spec] * 2,
        out_specs=(any_spec, any_spec, any_spec, any_spec, vmem_spec),
        scratch_shapes=[pltpu.VMEM((2 * (rows + tok), hd), bf), dma((2, 4))],
    )(out, dq, dk, dv, hs, head_scale.reshape(1, nk * group))
    return (
        out.reshape(queries.shape),
        dq.reshape(queries.shape),
        dk.reshape(keys.shape),
        dv.reshape(values.shape),
        d_head_scale.reshape(head_scale.shape),
    )


def solution(mesh):
    return jax.shard_map(
        local,
        mesh=mesh,
        in_specs=(
            P("dp", "ctx", "kvh", None),
            P("dp", "ctx", "kvh", None),
            P("dp", "ctx", "kvh", None),
            P("dp", "ctx", "kvh", None),
            P(),
            P("dp", None),
            P(),
        ),
        out_specs=(
            P("dp", "ctx", "kvh", None),
            P("dp", "ctx", "kvh", None),
            P("dp", "ctx", "kvh", None),
            P("dp", "ctx", "kvh", None),
            P(),
        ),
        check_vma=False,
    )
```

```python
import functools
import math

import jax
import jax.numpy as jnp
from jax import lax
from jax.experimental import pallas as pl
from jax.experimental.pallas import tpu as pltpu
from jax.sharding import PartitionSpec as P

MESH = pl.DeviceIdType.MESH
masked_low = -1e30
hidden = -16384.0
NX = 4
X_LAG = 2
RELAY_LAG = 2
ROW_LAG = 4


def nt_dot(a, b):
    return lax.dot_general(a, b, (((1,), (1,)), ((), ())), preferred_element_type=jnp.float32)


def nn_dot(a, b):
    return lax.dot_general(a, b, (((1,), (0,)), ((), ())), preferred_element_type=jnp.float32)


def xor_index(a, b, count):
    total, bit = 0, 1
    while bit < count:
        total = total + (lax.rem(lax.div(a, bit) + lax.div(b, bit), 2)) * bit
        bit *= 2
    return total


def kernel(
    group, tok, hd, docs, nk, nd,
    q_hbm, k_hbm, v_hbm, do_hbm, scale_ref, docs_ref, span_ref,
    out_hbm, dq_hbm, dk_ref, dv_ref, hs_ref,
    q_s, qf_s, do_s, qt_s, dot_s, kv, s_s, dp_s, row_lo, row_hi, m_s, l_s, wu_s, wd_s, wdu_s, acc_s,
    out_s, dq_s, p_s, ds_s, part, rxa, rxc, rz, h_own, h_kv, h_plane, h_own_all, h_line, h_gate, h_hi, h_all,
    in_sem, g_recv, gz_send, gx_send, gr_send, a_send, a_recv,
    c_send, c_recv, z_send, z_recv,
    h_send, hk_recv, hp_recv, hl_recv, hh_recv, ha_recv,
):
    nz = lax.axis_size("ctx") // NX
    rows = group * tok
    chunk = NX * tok
    span = tok // 2
    tile = min(512, rows)
    tiles = rows // tile
    me = lax.axis_index("ctx")
    ki, di = lax.axis_index("kvh"), lax.axis_index("dp")
    z, x = lax.div(me, NX), lax.rem(me, NX)
    pair = lax.div(z, 2)
    zp = z + 1 - 2 * lax.rem(z, 2)
    xr, xl, xo = lax.rem(x + 1, NX), lax.rem(x + 3, NX), lax.rem(x + 2, NX)

    def row(j):
        return xor_index(z, jnp.int32(j), nz)

    def x_dev(shift):
        return {"ctx": z * NX + lax.rem(x + shift, NX)}

    right, left = x_dev(1), x_dev(3)
    mate = {"ctx": zp * NX + x}
    up = {"ctx": lax.rem(z + 2, nz) * NX + x}
    down = {"ctx": lax.rem(z + nz - 2, nz) * NX + x}

    cores = min(2, nd)
    core, hi = lax.rem(di, cores), lax.div(di, cores)
    gate = (nz - 1) * (1 - hi)
    at_gate = z == gate

    def kv_dev(t):
        return {"kvh": lax.rem(ki + t, nk)}

    def plane_dev(t):
        to_core = lax.rem(core + t // NX, cores)
        return {"ctx": z * NX + lax.rem(x + t % NX, NX), "dp": hi * cores + to_core}

    def line_dev(zz):
        return {"ctx": zz * NX + x}

    across = {"ctx": (nz - 1) * hi * NX + x, "dp": lax.rem(di + cores, nd)}

    k_in = pltpu.make_async_copy(k_hbm, kv.at[z, x, 0], in_sem.at[0])
    v_in = pltpu.make_async_copy(v_hbm, kv.at[z, x, 1], in_sem.at[1])
    q_in = pltpu.make_async_copy(q_hbm, q_s, in_sem.at[2])
    do_in = pltpu.make_async_copy(do_hbm, do_s, in_sem.at[3])
    for load in (k_in, v_in, q_in, do_in):
        load.start()

    barrier = pltpu.get_barrier_semaphore()
    partners = [mate] + [kv_dev(t) for t in range(1, nk)]
    partners = partners + [plane_dev(t) for t in range(1, NX * cores)]

    def greet(partner):
        pl.semaphore_signal(barrier, inc=1, device_id=partner, device_id_type=MESH)

    for partner in partners:
        greet(partner)

    @pl.when(z < nz - 2)
    def _():
        greet(up)

    @pl.when(z >= 2)
    def _():
        greet(down)

    inner = jnp.where((z >= 2) & (z < nz - 2), 1, 0)
    if nd > cores:

        @pl.when(at_gate)
        def _():
            greet(across)

        inner = inner + jnp.where(at_gate, 1, 0)
    pl.semaphore_wait(barrier, len(partners) + 1 + inner)

    def remote(src, dst, send_sem, recv_sem, device):
        return pltpu.make_async_remote_copy(
            src_ref=src,
            dst_ref=dst,
            send_sem=send_sem,
            recv_sem=recv_sem,
            device_id=device,
            device_id_type=MESH,
        )

    def piece_copy(zb, bx, piece, send_sem, device):
        at = (zb, bx, piece)
        return remote(kv.at[at], kv.at[at], send_sem, g_recv.at[at], device)

    def line_copy(origin, side, piece):
        sem = gz_send.at[side, origin, piece]
        return piece_copy(origin, x, piece, sem, up if side == 0 else down)

    def mate_copy(origin, piece):
        return piece_copy(origin, x, piece, gz_send.at[2, origin, piece], mate)

    def x_copy(zb, bx, side, piece):
        sem = gx_send.at[side, zb, piece]
        return piece_copy(zb, bx, piece, sem, right if side == 0 else left)

    def relay_copy(zb, bx, side):
        at = (zb, bx, side)
        return remote(
            kv.at[at], kv.at[at], gr_send.at[side, zb], g_recv.at[at], right if side == 0 else left
        )

    def x_sends(zb):
        for side, piece in ((0, 0), (1, 1), (0, 1), (1, 0)):
            x_copy(zb, x, side, piece).start()

    def relays(zb):
        x_copy(zb, xl, 0, 0).wait_recv()
        relay_copy(zb, xl, 0).start()
        x_copy(zb, xr, 1, 1).wait_recv()
        relay_copy(zb, xr, 1).start()

    def row_waits(zb):
        x_copy(zb, xl, 0, 1).wait_recv()
        x_copy(zb, xr, 1, 0).wait_recv()
        relay_copy(zb, xo, 0).wait_recv()
        relay_copy(zb, xo, 1).wait_recv()

    def forward_line(origin, side, piece):
        @pl.when((z < nz - 2) if side == 0 else (z >= 2))
        def _():
            line_copy(origin, side, piece).start()

    def line_step(e):
        for piece in range(2):
            if e == 1:
                mate_copy(zp, piece).wait_recv()
            else:

                @pl.when(zp >= 2 * (e - 1))
                def _():
                    mate_copy(zp - 2 * (e - 1), piece).wait_recv()

                @pl.when(zp + 2 * (e - 1) < nz)
                def _():
                    mate_copy(zp + 2 * (e - 1), piece).wait_recv()

        x_sends(row(2 * e - 1))
        if e < nz // 2:
            for piece in range(2):

                @pl.when(z >= 2 * e)
                def _():
                    line_copy(z - 2 * e, 0, piece).wait_recv()
                    forward_line(z - 2 * e, 0, piece)
                    mate_copy(z - 2 * e, piece).start()

                @pl.when(z + 2 * e < nz)
                def _():
                    line_copy(z + 2 * e, 1, piece).wait_recv()
                    forward_line(z + 2 * e, 1, piece)
                    mate_copy(z + 2 * e, piece).start()

            x_sends(row(2 * e))

    k_in.wait()
    forward_line(z, 0, 0)
    forward_line(z, 1, 0)
    v_in.wait()
    forward_line(z, 0, 1)
    forward_line(z, 1, 1)
    mate_copy(z, 0).start()
    mate_copy(z, 1).start()
    x_sends(z)

    head0 = ki * group
    sub = lax.broadcasted_iota(jnp.int32, (group, hd), 0)
    scale8 = jnp.zeros((group, hd), jnp.float32)
    for h in range(group):
        scale8 = jnp.where(sub == h, scale_ref[head0 + h], scale8)
    factor8 = scale8 * (1.0 / math.sqrt(hd))

    def per_row(tile8):
        return jnp.broadcast_to(tile8[None], (tile // group, group, hd)).reshape(tile, hd)

    bounds = []
    running = jnp.int32(0)
    for d in range(docs):
        running = running + docs_ref[0, d]
        bounds.append(running)
    first_span, second_span = span_ref[2 * me], span_ref[2 * me + 1]

    blocks = span_ref.shape[0]
    lane1 = lax.broadcasted_iota(jnp.int32, (1, hd), 1)
    doc_low = jnp.full((1, hd), 1 << 30, jnp.int32)
    doc_high = jnp.zeros((1, hd), jnp.int32)
    for d in range(docs):
        doc_low = jnp.where(lane1 == blocks + d, bounds[d - 1] if d else 0, doc_low)
        doc_high = jnp.where(lane1 == blocks + d, bounds[d], doc_high)
    doc_lane = (lane1 >= blocks) & (lane1 < blocks + docs)

    def row_values(r, carry):
        base = r * tile
        token = (lax.broadcasted_iota(jnp.int32, (tile, hd), 0) + base) // group
        place = jnp.where(token < span, first_span * span, second_span * span - span) + token
        low = jnp.zeros_like(place)
        for bound in bounds:
            low = jnp.maximum(low, jnp.where(place >= bound, bound, 0))
        at = pl.ds(pl.multiple_of(base, tile), tile)
        row_hi[at] = place
        lane = lax.broadcasted_iota(jnp.int32, (tile, hd), 1)
        later = (lane < blocks) & (lane * span > place)
        other = doc_lane & ((place < doc_low) | (place >= doc_high))
        qf_s[at] = jnp.where(later | other, hidden, 0.0).astype(jnp.bfloat16)
        row_lo[at] = low
        m_s[at] = jnp.full((tile, hd), masked_low, jnp.float32)
        for total in (l_s, wu_s, wd_s, wdu_s, acc_s):
            total[at] = jnp.zeros((tile, hd), jnp.float32)
        return carry

    lax.fori_loop(0, tiles, row_values, 0)
    q_in.wait()
    do_in.wait()

    def chunk_rows(zb, which):
        return kv[zb, :, which].reshape(chunk, hd)

    def forward_chunk(i, zb, own):
        key_rows, value_rows = chunk_rows(zb, 0), chunk_rows(zb, 1)
        lane = lax.broadcasted_iota(jnp.int32, (group, tok), 1)
        key_lane = lax.broadcasted_iota(jnp.int32, (tok, hd), 1)
        key_row = lax.broadcasted_iota(jnp.int32, (tok, hd), 0)
        places, features = [], []
        for b in range(NX):
            owner = zb * NX + b
            lower, upper = span_ref[owner * 2], span_ref[owner * 2 + 1]
            block = jnp.where(key_row < span, lower, upper)
            key_place = block * span + jnp.where(key_row < span, key_row, key_row - span)
            marked = (key_lane == block) | ((key_place >= doc_low) & (key_place < doc_high))
            features.append(jnp.where(marked, 1.0, 0.0).astype(jnp.bfloat16))
            place = jnp.where(lane < span, lower * span, upper * span - span) + lane
            places.append(
                jnp.broadcast_to(place[None], (tile // group, group, tok)).reshape(tile, tok)
            )
        key_rows = jnp.concatenate([key_rows, jnp.concatenate(features, axis=0)], axis=1)
        factor = per_row(factor8)
        for r in range(tiles):
            at = slice(r * tile, (r + 1) * tile)
            raw = nt_dot(jnp.concatenate([q_s[at], qf_s[at]], axis=1), key_rows)
            low, high = row_lo[at], row_hi[at]
            scores = []
            for b in range(NX):
                score = raw[:, b * tok : (b + 1) * tok] * factor
                if own:
                    visible = (places[b] >= low) & (places[b] <= high)
                    score = jnp.where(visible, score, masked_low)
                s_s[i, at, b * tok : (b + 1) * tok] = score
                scores.append(score)
            peak = jnp.maximum(
                jnp.maximum(scores[0], scores[1]), jnp.maximum(scores[2], scores[3])
            )
            old = m_s[at]
            new = jnp.maximum(old, jnp.max(peak, axis=1, keepdims=True))
            m_s[at] = new
            shift = new - old
            alpha = jnp.exp(old - new)
            d_prob = nt_dot(do_s[at], value_rows)
            w_sum, wu_sum, wd_sum, wdu_sum = [jnp.zeros((tile, tok), jnp.float32)] * 4
            for b in range(NX):
                cols = slice(b * tok, (b + 1) * tok)
                below = scores[b] - new
                weight = jnp.exp(below)
                d_here = d_prob[:, cols]
                p_s[at, cols] = weight.astype(jnp.bfloat16)
                dp_s[i, at, cols] = d_here
                weighted = weight * d_here
                w_sum, wu_sum = w_sum + weight, wu_sum + weight * below
                wd_sum, wdu_sum = wd_sum + weighted, wdu_sum + weighted * below
            w_old, wd_old = l_s[at], wd_s[at]
            wu_s[at] = alpha * (wu_s[at] - shift * w_old) + wu_sum
            wdu_s[at] = alpha * (wdu_s[at] - shift * wd_old) + wdu_sum
            l_s[at] = alpha * w_old + w_sum
            wd_s[at] = alpha * wd_old + wd_sum
            acc_s[at] = acc_s[at] * alpha
        acc_s[...] = acc_s[...] + nn_dot(p_s[...], value_rows)

    def gather_step(i, carry):
        @pl.when(i == 0)
        def _():
            for r in range(tiles):
                at = slice(r * tile, (r + 1) * tile)
                qt_s[:, at] = q_s[at].astype(jnp.float32).T.astype(jnp.bfloat16)
                dot_s[:, at] = do_s[at].astype(jnp.float32).T.astype(jnp.bfloat16)

        for e in range(1, nz // 2 + 1):

            @pl.when(i == 2 * e - 1)
            def _():
                line_step(e)

        @pl.when((i >= RELAY_LAG) & (i < nz + RELAY_LAG))
        def _():
            relays(row(i - RELAY_LAG))

        @pl.when(i >= ROW_LAG)
        def _():
            zb = row(i - ROW_LAG)
            row_waits(zb)

            @pl.when(i == ROW_LAG)
            def _():
                forward_chunk(0, zb, True)

            @pl.when(i > ROW_LAG)
            def _():
                forward_chunk(i - ROW_LAG, zb, False)

        return carry

    lax.fori_loop(0, nz + ROW_LAG, gather_step, 0)

    def finish_rows(r, hs_total):
        at = pl.ds(pl.multiple_of(r * tile, tile), tile)
        weights = l_s[at]
        total = jnp.sum(weights, axis=1, keepdims=True)
        log_total = jnp.log(total)
        out_rows = (acc_s[at] / total).astype(jnp.bfloat16)
        out_s[at] = out_rows
        m_s[at] = m_s[at] + log_total
        product = do_s[at].astype(jnp.float32) * out_rows.astype(jnp.float32)
        delta = jnp.sum(product, axis=1, keepdims=True)
        terms = wdu_s[at] - delta * wu_s[at] - log_total * (wd_s[at] - delta * weights)
        l_s[at] = jnp.broadcast_to(delta, (tile, hd))
        acc_s[at] = jnp.zeros((tile, hd), jnp.float32)
        return hs_total + jnp.sum((terms / total).reshape(tile // group, group, hd), axis=0)

    no_terms = jnp.zeros((group, hd), jnp.float32)
    h_own[...] = lax.fori_loop(0, tiles, finish_rows, no_terms)
    out_copy = pltpu.make_async_copy(out_s, out_hbm, in_sem.at[0])
    out_copy.start()

    def kv_share(t):
        return remote(h_own, h_kv.at[ki], h_send.at[0, t], hk_recv.at[ki], kv_dev(t))

    def plane_share(t):
        slot = core * NX + x
        return remote(h_kv, h_plane.at[slot], h_send.at[1, t], hp_recv.at[slot], plane_dev(t))

    def line_share():
        return remote(h_own_all, h_line.at[z], h_send.at[2, 0], hl_recv.at[z], line_dev(gate))

    def across_share():
        return remote(h_gate, h_hi.at[hi], h_send.at[3, 0], hh_recv.at[hi], across)

    def all_share(zz):
        return remote(h_all, h_all, h_send.at[4, zz], ha_recv.at[0], line_dev(zz))

    def arrived(buffer, sem):
        remote(buffer, buffer, sem, sem, right).wait_recv()

    for t in range(1, nk):
        kv_share(t).start()

    def share_plane():
        h_kv[ki] = h_own[...]
        for t in range(1, nk):
            slot = lax.rem(ki + t, nk)
            arrived(h_kv.at[slot], hk_recv.at[slot])
        for t in range(1, NX * cores):
            plane_share(t).start()

    def share_line():
        h_plane[core * NX + x] = h_kv[...]
        for t in range(1, NX * cores):
            slot = lax.rem(core + t // NX, cores) * NX + lax.rem(x + t % NX, NX)
            arrived(h_plane.at[slot], hp_recv.at[slot])
        total = h_plane[0]
        for t in range(1, NX * cores):
            total = total + h_plane[t]
        h_own_all[...] = total

        @pl.when(jnp.logical_not(at_gate))
        def _():
            line_share().start()

    def line_total():
        h_line[z] = h_own_all[...]

        def more(j, total):
            zz = lax.rem(gate + j, nz)
            arrived(h_line.at[zz], hl_recv.at[zz])
            return total

        lax.fori_loop(1, nz, more, 0)
        total = h_line[0]
        for zz in range(1, nz):
            total = total + h_line[zz]
        h_gate[...] = total

    def share_across():
        line_total()
        if nd > cores:
            across_share().start()

    def share_all():
        if nd > cores:
            arrived(h_hi.at[1 - hi], hh_recv.at[1 - hi])
            h_hi[hi] = h_gate[...]
            h_all[...] = h_hi[0] + h_hi[1]
        else:
            h_all[...] = h_gate[...]
        for j in range(1, nz):
            all_share(lax.rem(gate + j, nz)).start()


    def a_copy(j, side):
        return remote(
            part.at[j, xo, side],
            rxa.at[j, side],
            a_send.at[j, side],
            a_recv.at[j, side],
            left if side == 0 else right,
        )

    def c_copy(j, side, piece):
        return remote(
            part.at[j, xl if side == 0 else xr, piece],
            rxc.at[j, side, piece],
            c_send.at[j, side, piece],
            c_recv.at[j, side, piece],
            left if side == 0 else right,
        )

    def line_sum(j, zb, side, piece):
        return remote(
            part.at[j, x, piece],
            rz.at[side, zb, piece],
            z_send.at[side, zb, piece],
            z_recv.at[side, zb, piece],
            up if side == 0 else down,
        )

    def mate_sum(j, zb, piece):
        return remote(
            part.at[j, x, piece],
            rz.at[2, zb, piece],
            z_send.at[2, zb, piece],
            z_recv.at[2, zb, piece],
            mate,
        )

    def add_bf(a, b):
        return (a.astype(jnp.float32) + b.astype(jnp.float32)).astype(jnp.bfloat16)

    def neighbour_sums(j):
        a_copy(j, 0).wait_recv()
        part[j, xl, 0] = add_bf(part[j, xl, 0], rxa[j, 0])
        c_copy(j, 0, 0).start()
        a_copy(j, 1).wait_recv()
        part[j, xr, 1] = add_bf(part[j, xr, 1], rxa[j, 1])
        c_copy(j, 1, 1).start()

    def column_sums(j):
        for side in range(2):
            for piece in range(2):
                c_copy(j, side, piece).wait_recv()
        total = part[j, x].astype(jnp.float32) + rxc[j, 0].astype(jnp.float32)
        total = total + rxc[j, 1].astype(jnp.float32)
        part[j, x] = total.astype(jnp.bfloat16)

    def to_mate(s):
        def send(target):
            for piece in range(2):
                at = 2 * xor_index(pair, target, nz // 2) + 1
                mate_sum(at, zp + 2 * (target - pair), piece).start()

        if s == 0:
            send(pair)
        else:

            @pl.when(pair + s < nz // 2)
            def _():
                send(pair + s)

            @pl.when(pair >= s)
            def _():
                send(pair - s)

    def along_line(s):
        for piece in range(2):
            for side, far in ((0, s), (1, -s)):

                @pl.when((pair + s < nz // 2) if side == 0 else (pair >= s))
                def _():
                    zb = z + 2 * far
                    at = 2 * xor_index(pair, pair + far, nz // 2)
                    mate_sum(at, zb, piece).wait_recv()
                    part[at, x, piece] = add_bf(part[at, x, piece], rz[2, zb, piece])

                    @pl.when((pair > 0) if side == 0 else (pair < nz // 2 - 1))
                    def _():
                        line_sum(at, zb, side, piece).wait_recv()
                        part[at, x, piece] = add_bf(part[at, x, piece], rz[side, zb, piece])

                    line_sum(at, zb, side, piece).start()

    def backward_chunk(i):
        key_rows = chunk_rows(row(i), 0)
        factor = per_row(factor8)
        for r in range(tiles):
            at = slice(r * tile, (r + 1) * tile)
            norm, delta = m_s[at], l_s[at]
            for b in range(NX):
                cols = slice(b * tok, (b + 1) * tok)
                prob = jnp.exp(s_s[i, at, cols] - norm)
                d_score = prob * ((dp_s[i, at, cols] - delta) * factor)
                p_s[at, cols] = prob.astype(jnp.bfloat16)
                ds_s[at, cols] = d_score.astype(jnp.bfloat16)
            acc_s[at] = acc_s[at] + nn_dot(ds_s[at], key_rows)
        d_key = nn_dot(qt_s[...], ds_s[...])
        d_value = nn_dot(dot_s[...], p_s[...])
        for b in range(NX):
            cols = slice(b * tok, (b + 1) * tok)
            part[i, b, 0] = d_key[:, cols].astype(jnp.bfloat16)
            part[i, b, 1] = d_value[:, cols].astype(jnp.bfloat16)

    def scatter_step(k, carry):
        @pl.when(k < nz)
        def _():
            j = nz - 1 - k
            backward_chunk(j)
            a_copy(j, 0).start()
            a_copy(j, 1).start()
            c_copy(j, 0, 1).start()
            c_copy(j, 1, 0).start()

        @pl.when(k == nz - 1)
        def _():
            for r in range(tiles):
                at = slice(r * tile, (r + 1) * tile)
                dq_s[at] = acc_s[at].astype(jnp.bfloat16)
            dq_copy.start()

        @pl.when((k >= X_LAG) & (k < nz + X_LAG))
        def _():
            neighbour_sums(nz - 1 - k + X_LAG)

        @pl.when(k >= 2 * X_LAG)
        def _():
            j = nz - 1 - k + 2 * X_LAG
            column_sums(j)

        for f in range(nz // 2):

            @pl.when(k == 2 * X_LAG + 2 * f)
            def _():
                if f > 0:
                    along_line(nz // 2 - f)
                to_mate(nz // 2 - 1 - f)

        @pl.when(k == 1)
        def _():
            share_plane()

        @pl.when(k == 4)
        def _():
            share_line()

        @pl.when((k == nz) & at_gate)
        def _():
            share_across()

        @pl.when((k == nz + 2) & at_gate)
        def _():
            share_all()

        return carry

    dq_copy = pltpu.make_async_copy(dq_s, dq_hbm, in_sem.at[1])
    lax.fori_loop(0, nz + 2 * X_LAG, scatter_step, 0)

    for piece in range(2):
        mate_sum(0, z, piece).wait_recv()
    part[0, x] = add_bf(part[0, x], rz[2, z])

    @pl.when(pair > 0)
    def _():
        for piece in range(2):
            line_sum(0, z, 0, piece).wait_recv()
        part[0, x] = add_bf(part[0, x], rz[0, z])

    @pl.when(pair < nz // 2 - 1)
    def _():
        for piece in range(2):
            line_sum(0, z, 1, piece).wait_recv()
        part[0, x] = add_bf(part[0, x], rz[1, z])

    dk_ref[...] = part[0, x, 0].astype(jnp.float32).T.astype(jnp.bfloat16)
    dv_ref[...] = part[0, x, 1].astype(jnp.float32).T.astype(jnp.bfloat16)

    @pl.when(jnp.logical_not(at_gate))
    def _():
        arrived(h_all, ha_recv.at[0])

    for kk in range(nk):
        hs_ref[kk * group : (kk + 1) * group] = h_all[kk]

    for t in range(1, nk):
        kv_share(t).wait_send()
    for t in range(1, NX * cores):
        plane_share(t).wait_send()

    @pl.when(at_gate)
    def _():
        if nd > cores:
            across_share().wait_send()
        for j in range(1, nz):
            all_share(lax.rem(gate + j, nz)).wait_send()

    @pl.when(jnp.logical_not(at_gate))
    def _():
        line_share().wait_send()

    def drain(j, carry):
        for side in range(2):
            relay_copy(j, xl, side).wait_send()
            a_copy(j, side).wait_send()
            for piece in range(2):
                x_copy(j, x, side, piece).wait_send()
                c_copy(j, side, piece).wait_send()
        same = lax.rem(z + j, 2) == 0
        for piece in range(2):

            @pl.when(same)
            def _():
                mate_copy(j, piece).wait_send()

                @pl.when((j <= z) & (z < nz - 2))
                def _():
                    line_copy(j, 0, piece).wait_send()

                @pl.when((j >= z) & (z >= 2))
                def _():
                    line_copy(j, 1, piece).wait_send()

                @pl.when(j > z)
                def _():
                    line_sum(0, j, 0, piece).wait_send()

                @pl.when(j < z)
                def _():
                    line_sum(0, j, 1, piece).wait_send()

            @pl.when(jnp.logical_not(same))
            def _():
                mate_sum(0, j, piece).wait_send()

        return carry

    lax.fori_loop(0, nz, drain, 0)
    out_copy.wait()
    dq_copy.wait()


def results(out_in, dq_in, dk_in, dv_in, hs_in, scale_in, out, dq, dk, dv, d_scale, buffers, sem):
    pairs = ((out_in, out), (dq_in, dq), (dk_in, dk), (dv_in, dv))
    rows = [pair[0].shape[0] for pair in pairs]
    views = [buffers.at[pl.ds(sum(rows[:i]), rows[i])] for i in range(4)]
    loads = [pltpu.make_async_copy(pairs[i][0], views[i], sem.at[0, i]) for i in range(4)]
    stores = [pltpu.make_async_copy(views[i], pairs[i][1], sem.at[1, i]) for i in range(4)]
    for load in loads:
        load.start()
    totals = jnp.sum(hs_in[...].T, axis=0, keepdims=True)
    scales = scale_in[...]
    d_scale[...] = totals / scales
    for load, store in zip(loads, stores):
        load.wait()
        store.start()
    for store in stores:
        store.wait()


def local(queries, keys, values, d_out, head_scale, doc_lengths, span_order):
    _, tok, group, hd = queries.shape
    nz = lax.axis_size("ctx") // NX
    nk, nd = lax.axis_size("kvh"), lax.axis_size("dp")
    rows, chunk = tok * group, NX * tok
    bf, f32, i32 = jnp.bfloat16, jnp.float32, jnp.int32
    any_spec = pl.BlockSpec(memory_space=pl.ANY)
    vmem_spec = pl.BlockSpec(memory_space=pltpu.VMEM)
    smem_spec = pl.BlockSpec(memory_space=pltpu.SMEM)
    dma = pltpu.SemaphoreType.DMA
    out, dq, dk, dv, hs = pl.pallas_call(
        functools.partial(kernel, group, tok, hd, doc_lengths.shape[1], nk, nd),
        out_shape=(
            jax.ShapeDtypeStruct((rows, hd), bf),
            jax.ShapeDtypeStruct((rows, hd), bf),
            jax.ShapeDtypeStruct((tok, hd), bf),
            jax.ShapeDtypeStruct((tok, hd), bf),
            jax.ShapeDtypeStruct((nk * group, tok), f32),
        ),
        in_specs=[any_spec] * 4 + [smem_spec] * 3,
        out_specs=(any_spec, any_spec, vmem_spec, vmem_spec, vmem_spec),
        scratch_shapes=[
            pltpu.VMEM((rows, hd), bf),
            pltpu.VMEM((rows, hd), bf),
            pltpu.VMEM((rows, hd), bf),
            pltpu.VMEM((hd, rows), bf),
            pltpu.VMEM((hd, rows), bf),
            pltpu.VMEM((nz, NX, 2, tok, hd), bf),
            pltpu.VMEM((nz, rows, chunk), f32),
            pltpu.VMEM((nz, rows, chunk), f32),
            pltpu.VMEM((rows, hd), i32),
            pltpu.VMEM((rows, hd), i32),
            pltpu.VMEM((rows, hd), f32),
            pltpu.VMEM((rows, hd), f32),
            pltpu.VMEM((rows, hd), f32),
            pltpu.VMEM((rows, hd), f32),
            pltpu.VMEM((rows, hd), f32),
            pltpu.VMEM((rows, hd), f32),
            pltpu.VMEM((rows, hd), bf),
            pltpu.VMEM((rows, hd), bf),
            pltpu.VMEM((rows, chunk), bf),
            pltpu.VMEM((rows, chunk), bf),
            pltpu.VMEM((nz, NX, 2, hd, tok), bf),
            pltpu.VMEM((nz, 2, hd, tok), bf),
            pltpu.VMEM((nz, 2, 2, hd, tok), bf),
            pltpu.VMEM((3, nz, 2, hd, tok), bf),
            pltpu.VMEM((group, hd), f32),
            pltpu.VMEM((nk, group, hd), f32),
            pltpu.VMEM((2 * NX, nk, group, hd), f32),
            pltpu.VMEM((nk, group, hd), f32),
            pltpu.VMEM((nz, nk, group, hd), f32),
            pltpu.VMEM((nk, group, hd), f32),
            pltpu.VMEM((2, nk, group, hd), f32),
            pltpu.VMEM((nk, group, hd), f32),
            dma((4,)),
            dma((nz, NX, 2)),
            dma((3, nz, 2)),
            dma((2, nz, 2)),
            dma((2, nz)),
            dma((nz, 2)),
            dma((nz, 2)),
            dma((nz, 2, 2)),
            dma((nz, 2, 2)),
            dma((3, nz, 2)),
            dma((3, nz, 2)),
            dma((5, 2 * NX)),
            dma((nk,)),
            dma((2 * NX,)),
            dma((nz,)),
            dma((2,)),
            dma((1,)),
        ],
        compiler_params=pltpu.CompilerParams(
            collective_id=0, has_side_effects=True, vmem_limit_bytes=60 * 1024 * 1024
        ),
    )(
        queries.reshape(rows, hd),
        keys.reshape(tok, hd),
        values.reshape(tok, hd),
        d_out.reshape(rows, hd),
        head_scale,
        doc_lengths,
        span_order,
    )
    out, dq, dk, dv, d_head_scale = pl.pallas_call(
        results,
        out_shape=(
            jax.ShapeDtypeStruct((rows, hd), bf),
            jax.ShapeDtypeStruct((rows, hd), bf),
            jax.ShapeDtypeStruct((tok, hd), bf),
            jax.ShapeDtypeStruct((tok, hd), bf),
            jax.ShapeDtypeStruct((1, nk * group), f32),
        ),
        in_specs=[any_spec] * 4 + [vmem_spec] * 2,
        out_specs=(any_spec, any_spec, any_spec, any_spec, vmem_spec),
        scratch_shapes=[pltpu.VMEM((2 * (rows + tok), hd), bf), dma((2, 4))],
    )(out, dq, dk, dv, hs, head_scale.reshape(1, nk * group))
    return (
        out.reshape(queries.shape),
        dq.reshape(queries.shape),
        dk.reshape(keys.shape),
        dv.reshape(values.shape),
        d_head_scale.reshape(head_scale.shape),
    )


def solution(mesh):
    return jax.shard_map(
        local,
        mesh=mesh,
        in_specs=(
            P("dp", "ctx", "kvh", None),
            P("dp", "ctx", "kvh", None),
            P("dp", "ctx", "kvh", None),
            P("dp", "ctx", "kvh", None),
            P(),
            P("dp", None),
            P(),
        ),
        out_specs=(
            P("dp", "ctx", "kvh", None),
            P("dp", "ctx", "kvh", None),
            P("dp", "ctx", "kvh", None),
            P("dp", "ctx", "kvh", None),
            P(),
        ),
        check_vma=False,
    )
```
